128 devices in a mesh: row: 16 (over z_hi, y, core), col: 8 (over x, z_lo).
Axes of the slice: x: 4, y: 4, z: 4 (z_hi: 2, z_lo: 2; z = z_hi * 2 + z_lo), core: 2. Of those that a mesh axis runs over, the one named last changes fastest.
Arguments:
- features: bfloat16 [32768, 256], P(('row', 'col')), may hold values from -6 to 6
- tile_vals: bfloat16 [16, 8, 256, 128, 128], P('row', 'col'), may hold values from -0.046875 to 0.046875
- tile_rows: int32 [16, 8, 256], P('row', 'col'), may hold values from 0 to 15, as said below
- tile_cols: int32 [16, 8, 256], P('row', 'col'), may hold values from 0 to 31
- tile_counts: int32 [16, 8], P('row', 'col'), may hold values from 96 to 256, as said below
- combine_weight: bfloat16 [512, 256], replicated, may hold values from -0.25 to 0.25
- cotangent: bfloat16 [32768, 256], P(('row', 'col')), may hold values from -6 to 6
Outputs:
- hidden: bfloat16 [32768, 256], P(('row', 'col'))
- grad_features: bfloat16 [32768, 256], P(('row', 'col'))
- grad_weight: float32 [512, 256], replicated
The draws below stay inside these ranges and needn't reach their ends.
Inputs may be any that keep to these rules, and one draw needn't show every extreme that they name: `tile_rows`: live slots of one device may name the same (tile row, tile column) pair more than once; such tiles add. Dead slots may hold any position. `tile_counts`: exactly one device has 256 live slots.
All inputs are finite; a program needn't handle non-finite values.
Results may differ from the reference program's by a relative error of at most 0.025.
Values may be sent and summed in bfloat16 or wider, within the bound.
No kernel may reach another device: no remote copies, remote signals or barrier semaphores. Data moves between devices by JAX's collectives and lax.ppermute only.
A program may use at most 128 MiB of HBM per device.

```python
import jax
import jax.numpy as jnp
from jax import lax

F = 256
SLICE = 256
MAXT = 256
NODES = 32768
N_ROW = 16
N_COL = 8


def draw_tile_rows(key, part):
    key = jax.random.fold_in(key, 11)
    span_rows = N_COL * SLICE // 128
    places = jax.random.randint(key, (N_ROW * N_COL, MAXT), 0, span_rows).astype(jnp.int32)
    places = places.at[0, 0].set(span_rows - 1)
    places = places.at[N_ROW * N_COL - 1, 0].set(0)
    return places.reshape(N_ROW, N_COL, MAXT).astype(jnp.int32)


def draw_tile_cols(key, part):
    key = jax.random.fold_in(key, 13)
    span_cols = N_ROW * SLICE // 128
    places = jax.random.randint(key, (N_ROW * N_COL, MAXT), 0, span_cols).astype(jnp.int32)
    places = places.at[0, 0].set(0)
    places = places.at[N_ROW * N_COL - 1, 0].set(span_cols - 1)
    return places.reshape(N_ROW, N_COL, MAXT).astype(jnp.int32)


def draw_tile_counts(key, part):
    key = jax.random.fold_in(key, 5)
    key_base, key_pick = jax.random.split(key)
    lowest = max(1, MAXT * 3 // 8)
    highest = max(lowest, MAXT * 3 // 4)
    base_counts = jax.random.randint(key_base, (N_ROW * N_COL,), lowest, highest + 1)
    chosen = jax.random.randint(key_pick, (), 0, N_ROW * N_COL)
    device_ids = jnp.arange(N_ROW * N_COL, dtype=jnp.int32)
    counts_all = jnp.where(device_ids == chosen, MAXT, base_counts)
    return counts_all.reshape(N_ROW, N_COL).astype(jnp.int32)


def levels(rng, extent, cuts, smallest, largest):
    loudness = 1.0
    for axis_at, blocks in cuts:
        draws = jax.random.uniform(jax.random.fold_in(jax.random.fold_in(rng, 6), axis_at), (blocks,), jnp.float32, smallest / len(cuts), largest / len(cuts))
        loudness = loudness * jnp.repeat(jnp.exp(draws), extent[axis_at] // blocks).reshape((-1,) + (1,) * (len(extent) - 1 - axis_at))
    return loudness


def noise(key, extent, width, most, cuts=(), held_as=jnp.bfloat16):
    drawn = width * jax.random.normal(key, extent, jnp.float32)
    if cuts:
        drawn = drawn * levels(key, extent, cuts, -0.22, 0.18)
    return jnp.clip(drawn, -most, most).astype(held_as)


def setup_inputs(seed: int = 0) -> dict:
    splits = jax.random.split(jax.random.key(seed), 8)
    features = noise(splits[0], (NODES, F), 1.0, 6.0, ((0, 128),))
    tile_vals = noise(splits[1], (N_ROW, N_COL, MAXT, 128, 128), (MAXT * 16384 // SLICE) ** -0.5, 0.046875, ((0, 16), (1, 8)))
    tile_rows = draw_tile_rows(jax.random.fold_in(splits[7], 71), 0)
    tile_cols = draw_tile_cols(jax.random.fold_in(splits[7], 71), 0)
    tile_counts = draw_tile_counts(jax.random.fold_in(splits[7], 71), 0)
    combine_weight = noise(splits[5], (2 * F, F), (2 * F) ** -0.5, 0.25)
    cotangent = noise(splits[6], (NODES, F), 1.0, 6.0, ((0, 128),))
    return {"features": features, "tile_vals": tile_vals, "tile_rows": tile_rows, "tile_cols": tile_cols, "tile_counts": tile_counts, "combine_weight": combine_weight, "cotangent": cotangent}


def propagate(left_source, right_source, tile_vals, tile_rows, tile_cols, tile_counts):
    feature_width = left_source.shape[1]
    block_rows = N_COL * SLICE
    block_cols = N_ROW * SLICE
    devices_all = N_ROW * N_COL
    column_view = left_source.reshape(N_ROW, N_COL, SLICE, feature_width).transpose(1, 0, 2, 3)
    column_view = column_view.reshape(N_COL, block_cols // 128, 128, feature_width)
    row_view = right_source.reshape(N_ROW, block_rows // 128, 128, feature_width)
    flat_vals = tile_vals.reshape(devices_all, MAXT, 128, 128)
    flat_rows = tile_rows.reshape(devices_all, MAXT).astype(jnp.int32)
    flat_cols = tile_cols.reshape(devices_all, MAXT).astype(jnp.int32)
    flat_counts = tile_counts.reshape(devices_all).astype(jnp.int32)

    def visit(running, pieces):
        into_rows, into_cols = running
        values, rows_here, cols_here, live_count, device = pieces
        row_id = device // N_COL
        col_id = device % N_COL
        live_mask = (jnp.arange(MAXT, dtype=jnp.int32) < live_count).astype(jnp.float32)
        tile_floats = values.astype(jnp.float32)
        left_feats = column_view[col_id][cols_here].astype(jnp.float32)
        right_feats = row_view[row_id][rows_here].astype(jnp.float32)
        forward_terms = jnp.einsum("tij,tjf->tif", tile_floats, left_feats) * live_mask[:, None, None]
        backward_terms = jnp.einsum("tij,tif->tjf", tile_floats, right_feats) * live_mask[:, None, None]
        into_rows = into_rows.at[row_id, rows_here].add(forward_terms)
        into_cols = into_cols.at[col_id, cols_here].add(backward_terms)
        return (into_rows, into_cols), None

    start_rows = jnp.zeros((N_ROW, block_rows // 128, 128, feature_width), jnp.float32)
    start_cols = jnp.zeros((N_COL, block_cols // 128, 128, feature_width), jnp.float32)
    device_ids = jnp.arange(devices_all, dtype=jnp.int32)
    (into_rows, into_cols), _ = lax.scan(visit, (start_rows, start_cols), (flat_vals, flat_rows, flat_cols, flat_counts, device_ids))
    total_rows = into_rows.reshape(-1, feature_width)
    total_cols = into_cols.reshape(N_COL, N_ROW, SLICE, feature_width).transpose(1, 0, 2, 3).reshape(-1, feature_width)
    return total_rows, total_cols


def reference(features, tile_vals, tile_rows, tile_cols, tile_counts, combine_weight, cotangent):
    inbound, outbound = propagate(features, features, tile_vals, tile_rows, tile_cols, tile_counts)
    joined = jnp.concatenate([inbound.astype(jnp.bfloat16), outbound.astype(jnp.bfloat16)], axis=1)
    pre_act = jnp.dot(joined, combine_weight, preferred_element_type=jnp.float32)
    hidden = jax.nn.silu(pre_act).astype(jnp.bfloat16)
    sigma = jax.nn.sigmoid(pre_act)
    slope = sigma * (1.0 + pre_act * (1.0 - sigma))
    grad_pre = (cotangent.astype(jnp.float32) * slope).astype(jnp.bfloat16)
    grad_joined = jnp.dot(grad_pre, combine_weight.T, preferred_element_type=jnp.float32)
    grad_in = grad_joined[:, :F].astype(jnp.bfloat16)
    grad_out = grad_joined[:, F:].astype(jnp.bfloat16)
    grad_weight = jnp.dot(joined.T, grad_pre, preferred_element_type=jnp.float32)
    back_rows, back_cols = propagate(grad_out, grad_in, tile_vals, tile_rows, tile_cols, tile_counts)
    grad_features = (back_rows + back_cols).astype(jnp.bfloat16)
    return hidden, grad_features, grad_weight
```

```python
import jax
import jax.numpy as jnp
from jax import lax
from jax.experimental import pallas as pl
from jax.experimental.pallas import tpu as pltpu
from jax.sharding import PartitionSpec as P

f32 = jnp.float32
bf16 = jnp.bfloat16
MIB = 1 << 20


def row_pairs(dz, dy, dc):
    return [
        (i, ((i >> 3) ^ dz) << 3 | (((i >> 1 & 3) + dy) % 4) << 1 | ((i & 1) ^ dc)) for i in range(16)
    ]


def col_pairs(dx, dz):
    return [(i, (((i >> 1) + dx) % 4) << 1 | ((i & 1) ^ dz)) for i in range(8)]


def row_move(value, dz, dy, dc):
    return lax.ppermute(value, "row", row_pairs(dz, dy, dc))


def col_move(value, dx, dz):
    return lax.ppermute(value, "col", col_pairs(dx, dz))


def places(tile_rows, tile_cols, live_count):
    r = lax.axis_index("row")
    c = lax.axis_index("col")
    slots = tile_rows.shape[0]
    slice_c = tile_rows >> 1
    slice_r = tile_cols >> 1
    kappa = (((slice_c >> 1) - (c >> 1)) & 3) << 1 | ((slice_c ^ c) & 1)
    rho = ((slice_r ^ r) & 1) << 3 | (((slice_r >> 1) - (r >> 1)) & 3) << 1 | (((slice_r ^ r) >> 3) & 1)
    key = rho << 5 | kappa << 2 | (tile_rows & 1) << 1 | (tile_cols & 1)
    index = jnp.arange(slots, dtype=jnp.int32)
    key = jnp.where(index < live_count, key, 512)
    unique = key * slots + index
    rank = jnp.sum((unique[None, :] < unique[:, None]).astype(jnp.int32), axis=1)
    hit = rank[:, None] == index[None, :]
    ordered = jnp.sum(jnp.where(hit, unique[:, None], 0), axis=0)
    order = ordered % slots
    place = ordered // slots
    same1 = jnp.concatenate([jnp.zeros((1,), jnp.bool_), place[1:] == place[:-1]])
    same2 = jnp.concatenate([jnp.zeros((2,), jnp.bool_), place[2:] == place[:-2]])
    seen = same1.astype(jnp.int32) + same2.astype(jnp.int32)
    return jnp.stack([order, place, seen])


def densify_kernel(count_ref, plan_ref, vals_ref, dense_ref, tiles, total, sem):
    copy = pltpu.make_async_copy(vals_ref, tiles, sem)
    copy.start()

    @pl.loop(0, 16)
    def _(rho):
        dense_ref[rho] = jnp.zeros(dense_ref.shape[1:], bf16)

    copy.wait()

    @pl.loop(0, count_ref[0])
    def _(k):
        slot = plan_ref[0, k]
        place = plan_ref[1, k]
        seen = plan_ref[2, k]
        rho = place >> 5
        at_row = pl.ds(pl.multiple_of(((place >> 1) & 15) * 128, 128), 128)
        at_col = pl.ds(pl.multiple_of((place & 1) * 128, 128), 128)

        @pl.when(seen == 0)
        def _():
            dense_ref[rho, at_row, at_col] = tiles[slot]

        @pl.when(seen > 0)
        def _():
            before = tiles[plan_ref[0, jnp.maximum(k - 1, 0)]].astype(f32)
            before = jnp.where(seen > 1, total[...], before)
            now = before + tiles[slot].astype(f32)
            total[...] = now
            dense_ref[rho, at_row, at_col] = now.astype(bf16)


def densify(slot_values, plan, live_count):
    slots = slot_values.shape[0]
    return pl.pallas_call(
        densify_kernel,
        grid_spec=pltpu.PrefetchScalarGridSpec(
            num_scalar_prefetch=2,
            grid=(),
            in_specs=[pl.BlockSpec(memory_space=pl.ANY)],
            out_specs=pl.BlockSpec(memory_space=pltpu.VMEM),
            scratch_shapes=[
                pltpu.VMEM((slots, 128, 128), bf16),
                pltpu.VMEM((128, 128), f32),
                pltpu.SemaphoreType.DMA,
            ],
        ),
        out_shape=jax.ShapeDtypeStruct((16, 2048, 256), bf16),
        compiler_params=pltpu.CompilerParams(vmem_limit_bytes=30 * MIB),
        name="densify",
    )(live_count.reshape(1), plan, slot_values)


def outbound_kernel(dense_ref, *refs):
    sources, far, near = refs[:4], refs[4:8], refs[8:12]
    for group in range(8):
        for half in range(2):
            rho = group * 2 + half
            total = jnp.zeros((256, 256), f32)
            for q in range(4):
                total = total + lax.dot_general(
                    dense_ref[rho, q * 512 : (q + 1) * 512, :],
                    sources[q][...],
                    (((0,), (0,)), ((), ())),
                    preferred_element_type=f32,
                )
            rows = slice(half * 256, half * 256 + 256)
            if group >= 4:
                far[group - 4][rows, :] = total.astype(bf16)
            else:
                near[group][rows, :] = total


def inbound_kernel(dense_ref, *refs):
    sources, outs = refs[:8], refs[8:12]
    for q in range(4):
        total = jnp.zeros((512, 256), f32)
        for p in range(8):
            for half in range(2):
                total = total + jnp.dot(
                    dense_ref[p * 2 + half, q * 512 : (q + 1) * 512, :],
                    sources[p][half * 256 : half * 256 + 256, :],
                    preferred_element_type=f32,
                )
        outs[q][...] = total.astype(outs[q].dtype)


def products(kernel, dense, sources, outs, name):
    whole = pl.BlockSpec(memory_space=pltpu.VMEM)
    return pl.pallas_call(
        kernel,
        in_specs=[whole] * (1 + len(sources)),
        out_specs=[whole] * len(outs),
        out_shape=outs,
        compiler_params=pltpu.CompilerParams(vmem_limit_bytes=30 * MIB),
        name=name,
    )(dense, *sources)


def spread(for_cols, for_rows):
    row_z = row_move(for_rows, 1, 0, 0)
    col_z = col_move(for_cols, 0, 1)
    row_pair = jnp.concatenate([for_rows, row_z], axis=0)
    col_pair = jnp.concatenate([for_cols, col_z], axis=0)
    by_col = [col_pair] + [col_move(col_pair, -dx, 0) for dx in (1, 2, 3)]
    by_row = [row_pair] + [row_move(row_pair, 0, -dy, 0) for dy in (1, 2, 3)]
    other = [row_move(piece, 0, 0, 1) for piece in by_row]
    return by_col, by_row + other


def fold_rows(far, near):
    other = [row_move(piece, 0, 0, 1) for piece in far]
    mine = [a + b.astype(f32) for a, b in zip(near, other)]
    arrived = [row_move(mine[dy].astype(bf16), 0, dy, 0) for dy in (1, 2, 3)]
    total = mine[0] + arrived[0].astype(f32) + arrived[1].astype(f32) + arrived[2].astype(f32)
    last = row_move(total[256:].astype(bf16), 1, 0, 0)
    return total[:256] + last.astype(f32)


def fold_cols(pieces):
    arrived = [col_move(pieces[dx], dx, 0) for dx in (1, 2, 3)]
    total = pieces[0] + arrived[0].astype(f32) + arrived[1].astype(f32) + arrived[2].astype(f32)
    last = col_move(total[256:].astype(bf16), 0, 1)
    return total[:256] + last.astype(f32)


def propagate(dense, for_cols, for_rows):
    by_col, by_row = spread(for_cols, for_rows)
    piece = lambda dtype: jax.ShapeDtypeStruct((512, 256), dtype)
    out = products(outbound_kernel, dense, by_col, [piece(bf16)] * 4 + [piece(f32)] * 4, "outbound")
    inn = products(inbound_kernel, dense, by_row, [piece(f32)] + [piece(bf16)] * 3, "inbound")
    return fold_cols(inn), fold_rows(out[:4], out[4:])


def middle_kernel(in_ref, out_ref, weight_ref, cot_ref, hidden_ref, grad_in_ref, grad_out_ref, term_ref):
    inbound = in_ref[...].astype(bf16)
    outbound = out_ref[...].astype(bf16)
    width = inbound.shape[1]
    upper = weight_ref[:width, :]
    lower = weight_ref[width:, :]
    pre_act = jnp.dot(inbound, upper, preferred_element_type=f32)
    pre_act = pre_act + jnp.dot(outbound, lower, preferred_element_type=f32)
    sigma = jax.nn.sigmoid(pre_act)
    hidden_ref[...] = (pre_act * sigma).astype(bf16)
    slope = sigma * (1.0 + pre_act * (1.0 - sigma))
    grad_pre = (cot_ref[...].astype(f32) * slope).astype(bf16)
    across = (((1,), (1,)), ((), ()))
    grad_in_ref[...] = lax.dot_general(grad_pre, upper, across, preferred_element_type=f32).astype(bf16)
    grad_out_ref[...] = lax.dot_general(grad_pre, lower, across, preferred_element_type=f32).astype(bf16)
    down = (((0,), (0,)), ((), ()))
    term_ref[:width, :] = lax.dot_general(inbound, grad_pre, down, preferred_element_type=f32)
    term_ref[width:, :] = lax.dot_general(outbound, grad_pre, down, preferred_element_type=f32)


def middle(inbound, outbound, weight, cotangent):
    whole = pl.BlockSpec(memory_space=pltpu.VMEM)
    slab = jax.ShapeDtypeStruct(cotangent.shape, bf16)
    return pl.pallas_call(
        middle_kernel,
        in_specs=[whole] * 4,
        out_specs=[whole] * 4,
        out_shape=[slab, slab, slab, jax.ShapeDtypeStruct(weight.shape, f32)],
        compiler_params=pltpu.CompilerParams(vmem_limit_bytes=16 * MIB),
        name="middle",
    )(inbound, outbound, weight, cotangent)


def body(features, tile_vals, tile_rows, tile_cols, tile_counts, combine_weight, cotangent):
    live_count = tile_counts[0, 0]
    plan = places(tile_rows[0, 0], tile_cols[0, 0], live_count)
    dense = densify(tile_vals[0, 0], plan, live_count)
    inbound, outbound = propagate(dense, features, features)
    hidden, grad_in, grad_out, term = middle(inbound, outbound, combine_weight, cotangent)
    grad_weight = lax.psum(term, ("row", "col"))
    back_inbound, back_outbound = propagate(dense, grad_in, grad_out)
    grad_features = (back_inbound + back_outbound).astype(bf16)
    return hidden, grad_features, grad_weight


def solution(mesh):
    slabs = P(("row", "col"), None)
    return jax.shard_map(
        body,
        mesh=mesh,
        in_specs=(
            slabs,
            P("row", "col", None, None, None),
            P("row", "col", None),
            P("row", "col", None),
            P("row", "col"),
            P(),
            slabs,
        ),
        out_specs=(slabs, slabs, P()),
        check_vma=False,
    )
```

```python
import jax
import jax.numpy as jnp
from jax import lax
from jax.experimental import pallas as pl
from jax.experimental.pallas import tpu as pltpu
from jax.sharding import PartitionSpec as P

f32 = jnp.float32
bf16 = jnp.bfloat16
MIB = 1 << 20


def row_pairs(dz, dy, dc):
    return [
        (i, ((i >> 3) ^ dz) << 3 | (((i >> 1 & 3) + dy) % 4) << 1 | ((i & 1) ^ dc)) for i in range(16)
    ]


def col_pairs(dx, dz):
    return [(i, (((i >> 1) + dx) % 4) << 1 | ((i & 1) ^ dz)) for i in range(8)]


def row_move(value, dz, dy, dc):
    return lax.ppermute(value, "row", row_pairs(dz, dy, dc))


def col_move(value, dx, dz):
    return lax.ppermute(value, "col", col_pairs(dx, dz))


def places(tile_rows, tile_cols, live_count):
    r = lax.axis_index("row")
    c = lax.axis_index("col")
    slots = tile_rows.shape[0]
    slice_c = tile_rows >> 1
    slice_r = tile_cols >> 1
    kappa = (((slice_c >> 1) - (c >> 1)) & 3) << 1 | ((slice_c ^ c) & 1)
    rho = ((slice_r ^ r) & 1) << 3 | (((slice_r >> 1) - (r >> 1)) & 3) << 1 | (((slice_r ^ r) >> 3) & 1)
    key = rho << 5 | kappa << 2 | (tile_rows & 1) << 1 | (tile_cols & 1)
    index = jnp.arange(slots, dtype=jnp.int32)
    key = jnp.where(index < live_count, key, 512)
    unique = key * slots + index
    rank = jnp.sum((unique[None, :] < unique[:, None]).astype(jnp.int32), axis=1)
    hit = rank[:, None] == index[None, :]
    ordered = jnp.sum(jnp.where(hit, unique[:, None], 0), axis=0)
    order = ordered % slots
    place = ordered // slots
    same1 = jnp.concatenate([jnp.zeros((1,), jnp.bool_), place[1:] == place[:-1]])
    same2 = jnp.concatenate([jnp.zeros((2,), jnp.bool_), place[2:] == place[:-2]])
    seen = same1.astype(jnp.int32) + same2.astype(jnp.int32)
    return jnp.stack([order, place, seen])


def densify_kernel(count_ref, plan_ref, tiles, dense_ref, total):
    @pl.loop(0, 16)
    def _(rho):
        dense_ref[rho] = jnp.zeros(dense_ref.shape[1:], bf16)

    @pl.loop(0, count_ref[0])
    def _(k):
        slot = plan_ref[0, k]
        place = plan_ref[1, k]
        seen = plan_ref[2, k]
        rho = place >> 5
        at_row = pl.ds(pl.multiple_of(((place >> 1) & 15) * 128, 128), 128)
        at_col = pl.ds(pl.multiple_of((place & 1) * 128, 128), 128)

        @pl.when(seen == 0)
        def _():
            dense_ref[rho, at_row, at_col] = tiles[slot]

        @pl.when(seen > 0)
        def _():
            before = tiles[plan_ref[0, jnp.maximum(k - 1, 0)]].astype(f32)
            before = jnp.where(seen > 1, total[...], before)
            now = before + tiles[slot].astype(f32)
            total[...] = now
            dense_ref[rho, at_row, at_col] = now.astype(bf16)


WHOLE = pl.BlockSpec(memory_space=pltpu.VMEM)
SCALAR = pl.BlockSpec(memory_space=pltpu.SMEM)


def kernel_call(kernel, name, specs, args, outs, flops, after=(), scratch=()):
    moved = sum(a.size * a.dtype.itemsize for a in (*args, *outs))
    used, skipped = len(args), len(args) + len(after)

    def run(*refs):
        kernel(*refs[:used], *refs[skipped:])

    return pl.pallas_call(
        run,
        in_specs=[*specs, *[pl.BlockSpec(memory_space=pl.ANY)] * len(after)],
        out_specs=[WHOLE] * len(outs),
        out_shape=outs,
        scratch_shapes=scratch,
        cost_estimate=pl.CostEstimate(flops=flops, bytes_accessed=moved, transcendentals=0),
        compiler_params=pltpu.CompilerParams(vmem_limit_bytes=8 * MIB),
        name=name,
    )(*args, *after)


def array(rows, dtype):
    return jax.ShapeDtypeStruct((rows, 256), dtype)


def densify(slot_values, plan, live_count, after):
    (dense,) = kernel_call(
        densify_kernel,
        "densify",
        [SCALAR, SCALAR, WHOLE],
        (live_count.reshape(1), plan, slot_values),
        [jax.ShapeDtypeStruct((16, 2048, 256), bf16)],
        0,
        after,
        [pltpu.VMEM((128, 128), f32)],
    )
    return dense


def column_sum(dense_ref, sources, rho):
    total = jnp.zeros((256, 256), f32)
    for q in range(4):
        total = total + lax.dot_general(
            dense_ref[rho, q * 512 : (q + 1) * 512, :],
            sources[q][...],
            (((0,), (0,)), ((), ())),
            preferred_element_type=f32,
        )
    return total


def row_sum(dense_ref, sources, q):
    total = jnp.zeros((512, 256), f32)
    for p in range(8):
        for half in range(2):
            total = total + jnp.dot(
                dense_ref[p * 2 + half, q * 512 : (q + 1) * 512, :],
                sources[p][half * 256 : half * 256 + 256, :],
                preferred_element_type=f32,
            )
    return total


def out_far_kernel(dense_ref, *refs):
    for part in range(8):
        rows = slice(part * 256, part * 256 + 256)
        refs[4][rows, :] = column_sum(dense_ref, refs[:4], 8 + part).astype(bf16)


def out_sent_kernel(dense_ref, *refs):
    sources, arrived, outs = refs[:4], refs[4], refs[5:]
    for part in range(2, 8):
        rows = slice(part * 256, part * 256 + 256)
        total = column_sum(dense_ref, sources, part) + arrived[rows, :].astype(f32)
        outs[part // 2 - 1][part % 2 * 256 : part % 2 * 256 + 256, :] = total.astype(bf16)


def in_sent_kernel(dense_ref, *refs):
    for q in (1, 2, 3):
        refs[7 + q][...] = row_sum(dense_ref, refs[:8], q).astype(bf16)


def own_kernel(dense_ref, *refs):
    by_col, by_row, arrived, in_own, out_own = refs[:4], refs[4:12], refs[12], refs[13], refs[14]
    for part in range(2):
        rows = slice(part * 256, part * 256 + 256)
        out_own[rows, :] = column_sum(dense_ref, by_col, part) + arrived[rows, :].astype(f32)
    in_own[...] = row_sum(dense_ref, by_row, 0)


def pair_up(for_cols, for_rows):
    row_z = row_move(for_rows, 1, 0, 0)
    col_z = col_move(for_cols, 0, 1)
    return jnp.concatenate([for_cols, col_z], axis=0), row_z


def spread(col_pair, row_sends):
    by_col = [col_pair] + [col_move(col_pair, -dx, 0) for dx in (1, 2, 3)]
    by_row = [row_sends[0]] + [row_move(row_sends[4 - dy], 0, -dy, 0) for dy in (1, 2, 3)]
    return by_col, by_row, [row_move(piece, 0, 0, 1) for piece in by_row]


def propagate(dense, by_col, by_row, other):
    per_slice = 2 * 2048 * 256 * 256
    wide = [WHOLE] * 20
    sums = lambda kernel, name, args, outs, slices, after=(): kernel_call(
        kernel, name, wide[: len(args)], args, outs, slices * per_slice, after
    )
    (far,) = sums(out_far_kernel, "out_far", (dense, *by_col), [array(2048, bf16)], 8, by_row[1:])
    arrived = row_move(far, 0, 0, 1)
    in_sent = sums(in_sent_kernel, "in_sent", (dense, *by_row, *other), [array(512, bf16)] * 3, 12)
    in_moved = [col_move(in_sent[dx - 1], dx, 0) for dx in (1, 2, 3)]
    out_sent = sums(
        out_sent_kernel, "out_sent", (dense, *by_col, arrived), [array(512, bf16)] * 3, 6, in_sent[:1]
    )
    out_moved = [row_move(out_sent[dy - 1], 0, dy, 0) for dy in (1, 2, 3)]
    in_own, out_own = sums(
        own_kernel,
        "own",
        (dense, *by_col, *by_row, *other, arrived),
        [array(512, f32)] * 2,
        6,
        out_sent[:1],
    )
    return in_own + sum_of(in_moved), out_own + sum_of(out_moved)


def sum_of(values):
    total = values[0].astype(f32)
    for value in values[1:]:
        total = total + value.astype(f32)
    return total


def owner(r, dz, dy, dc):
    return ((r >> 3) ^ dz) << 3 | (((r >> 1) + dy) & 3) << 1 | ((r & 1) ^ dc)


def middle_kernel(
    r_ref,
    in_own,
    in_last,
    out_own,
    out_last,
    weight_ref,
    cot_ref,
    hidden_ref,
    grad_in_ref,
    pack_ref,
    kept_ref,
    term,
):
    inbound = (in_own[...] + in_last[...].astype(f32)).astype(bf16)
    outbound = (out_own[...] + out_last[...].astype(f32)).astype(bf16)
    width = inbound.shape[1]
    upper = weight_ref[:width, :]
    lower = weight_ref[width:, :]
    pre_act = jnp.dot(inbound, upper, preferred_element_type=f32)
    pre_act = pre_act + jnp.dot(outbound, lower, preferred_element_type=f32)
    sigma = jax.nn.sigmoid(pre_act)
    hidden_ref[...] = (pre_act * sigma).astype(bf16)
    slope = sigma * (1.0 + pre_act * (1.0 - sigma))
    grad_pre = (cot_ref[...].astype(f32) * slope).astype(bf16)
    across = (((1,), (1,)), ((), ()))
    grad_in_ref[...] = lax.dot_general(grad_pre, upper, across, preferred_element_type=f32).astype(bf16)
    grad_out = lax.dot_general(grad_pre, lower, across, preferred_element_type=f32)
    pack_ref[:256, :] = grad_out.astype(bf16)
    down = (((0,), (0,)), ((), ()))
    term[:width, :] = lax.dot_general(inbound, grad_pre, down, preferred_element_type=f32)
    term[width:, :] = lax.dot_general(outbound, grad_pre, down, preferred_element_type=f32)
    for dy in range(4):
        for dc in range(2):
            first = (dy * 2 + dc) * 32
            at = lambda dz: pl.ds(pl.multiple_of(owner(r_ref[0], dz, dy, dc) * 32, 32), 32)
            kept_ref[first : first + 32, :] = term[at(0), :]
            pack_ref[256 + first : 288 + first, :] = term[at(1), :].astype(bf16)


def middle(r, terms, weight, cotangent):
    return kernel_call(
        middle_kernel,
        "middle",
        [SCALAR] + [WHOLE] * 6,
        (r, *terms, weight, cotangent),
        [array(256, bf16), array(256, bf16), array(512, bf16), array(256, f32)],
        6 * 256 * 512 * 256,
        (),
        [pltpu.VMEM((512, 256), f32)],
    )


def weight_sum(total):
    total = total[:32] + row_move(total[32:].astype(bf16), 0, 0, 1).astype(f32)
    mine = total.astype(bf16)
    one, two, three = (col_move(mine, -dx, 0) for dx in (1, 2, 3))
    total = sum_of([mine, two]) + sum_of([one, three])
    mine = total.astype(bf16)
    return sum_of([mine, col_move(mine, 0, 1)]).astype(bf16)


def place_kernel(r_ref, same_ref, other_ref, out_ref):
    for dc, ref in ((0, same_ref), (1, other_ref)):
        for dz in range(2):
            for dy in range(4):
                at = (dz * 4 + dy) * 32
                to = pl.ds(pl.multiple_of(owner(r_ref[0], dz, dy, dc) * 32, 32), 32)
                out_ref[to, :] = ref[at : at + 32, :].astype(f32)


def body(features, tile_vals, tile_rows, tile_cols, tile_counts, combine_weight, cotangent):
    live_count = tile_counts[0, 0]
    r = lax.axis_index("row").astype(jnp.int32).reshape(1)
    plan = places(tile_rows[0, 0], tile_cols[0, 0], live_count)

    col_pair, row_z = pair_up(features, features)
    row_pair = jnp.concatenate([features, row_z], axis=0)
    dense = densify(tile_vals[0, 0], plan, live_count, (col_pair, row_pair))
    in_total, out_total = propagate(dense, *spread(col_pair, [row_pair] * 4))
    in_last = col_move(in_total[256:].astype(bf16), 0, 1)
    out_last = row_move(out_total[256:].astype(bf16), 1, 0, 0)
    terms = (in_total[:256], in_last, out_total[:256], out_last)
    hidden, grad_in, pack, kept = middle(r, terms, combine_weight, cotangent)

    col_pair, row_z = pair_up(grad_in, pack)
    row_pair = jnp.concatenate([pack[:256], row_z[:256]], axis=0)
    part = kept + row_z[256:].astype(f32)
    cut = part.astype(bf16)
    row_sends = [jnp.concatenate([row_pair, cut[dy * 64 : dy * 64 + 64]], axis=0) for dy in (1, 2, 3)]
    by_col, by_row, other = spread(col_pair, [row_pair] + row_sends)
    mine = weight_sum(part[:64] + sum_of([piece[512:] for piece in by_row[1:]]))
    in_total, out_total = propagate(dense, by_col, by_row, other)
    ring = jnp.concatenate([mine] + [row_move(mine, 0, -dy, 0) for dy in (1, 2, 3)], axis=0)
    in_last = col_move(in_total[256:].astype(bf16), 0, 1)
    out_last = row_move(jnp.concatenate([out_total[256:].astype(bf16), ring], axis=0), 1, 0, 0)
    plane = jnp.concatenate([ring, out_last[256:]], axis=0)
    (grad_weight,) = kernel_call(
        place_kernel,
        "place",
        [SCALAR, WHOLE, WHOLE],
        (r, plane, row_move(plane, 0, 0, 1)),
        [array(512, f32)],
        0,
    )
    grad_features = sum_of([in_total[:256], in_last, out_total[:256], out_last[:256]]).astype(bf16)
    return hidden, grad_features, grad_weight


def solution(mesh):
    slabs = P(("row", "col"), None)
    return jax.shard_map(
        body,
        mesh=mesh,
        in_specs=(
            slabs,
            P("row", "col", None, None, None),
            P("row", "col", None),
            P("row", "col", None),
            P("row", "col"),
            P(),
            slabs,
        ),
        out_specs=(slabs, slabs, P()),
        check_vma=False,
    )
```

```python
import jax
import jax.numpy as jnp
from jax import lax
from jax.experimental import pallas as pl
from jax.experimental.pallas import tpu as pltpu
from jax.sharding import PartitionSpec as P

f32 = jnp.float32
bf16 = jnp.bfloat16
MIB = 1 << 20


def row_pairs(dz, dy, dc):
    return [
        (i, ((i >> 3) ^ dz) << 3 | (((i >> 1 & 3) + dy) % 4) << 1 | ((i & 1) ^ dc)) for i in range(16)
    ]


def col_pairs(dx, dz):
    return [(i, (((i >> 1) + dx) % 4) << 1 | ((i & 1) ^ dz)) for i in range(8)]


def row_move(value, dz, dy, dc):
    return lax.ppermute(value, "row", row_pairs(dz, dy, dc))


def col_move(value, dx, dz):
    return lax.ppermute(value, "col", col_pairs(dx, dz))


def places(tile_rows, tile_cols, live_count):
    r = lax.axis_index("row")
    c = lax.axis_index("col")
    slots = tile_rows.shape[0]
    slice_c = tile_rows >> 1
    slice_r = tile_cols >> 1
    kappa = ((slice_c ^ c) & 1) << 2 | (((slice_c >> 1) - (c >> 1)) & 3)
    rho = ((slice_r ^ r) & 1) << 3 | (((slice_r >> 1) - (r >> 1)) & 3) << 1 | (((slice_r ^ r) >> 3) & 1)
    key = rho << 5 | kappa << 2 | (tile_rows & 1) << 1 | (tile_cols & 1)
    index = jnp.arange(slots, dtype=jnp.int32)
    key = jnp.where(index < live_count, key, 512)
    unique = key * slots + index
    rank = jnp.sum((unique[None, :] < unique[:, None]).astype(jnp.int32), axis=1)
    hit = rank[:, None] == index[None, :]
    ordered = jnp.sum(jnp.where(hit, unique[:, None], 0), axis=0)
    order = ordered % slots
    place = ordered // slots
    same1 = jnp.concatenate([jnp.zeros((1,), jnp.bool_), place[1:] == place[:-1]])
    same2 = jnp.concatenate([jnp.zeros((2,), jnp.bool_), place[2:] == place[:-2]])
    seen = same1.astype(jnp.int32) + same2.astype(jnp.int32)
    return jnp.stack([order, place, seen])


def load_kernel(vals_ref, tiles_ref, dense_ref, sem):
    copy = pltpu.make_async_copy(vals_ref, tiles_ref, sem)
    copy.start()

    @pl.loop(0, 16)
    def _(rho):
        dense_ref[rho] = jnp.zeros(dense_ref.shape[1:], bf16)

    copy.wait()


def densify_kernel(count_ref, plan_ref, tiles, zeros_ref, dense_ref, total):
    del zeros_ref

    @pl.loop(0, count_ref[0])
    def _(k):
        slot = plan_ref[0, k]
        place = plan_ref[1, k]
        seen = plan_ref[2, k]
        rho = place >> 5
        at_row = pl.ds(pl.multiple_of(((place >> 1) & 15) * 128, 128), 128)
        at_col = pl.ds(pl.multiple_of((place & 1) * 128, 128), 128)

        @pl.when(seen == 0)
        def _():
            dense_ref[rho, at_row, at_col] = tiles[slot]

        @pl.when(seen > 0)
        def _():
            before = tiles[plan_ref[0, jnp.maximum(k - 1, 0)]].astype(f32)
            before = jnp.where(seen > 1, total[...], before)
            now = before + tiles[slot].astype(f32)
            total[...] = now
            dense_ref[rho, at_row, at_col] = now.astype(bf16)


WHOLE = pl.BlockSpec(memory_space=pltpu.VMEM)
SCALAR = pl.BlockSpec(memory_space=pltpu.SMEM)


def kernel_call(kernel, name, specs, args, outs, flops, after=(), scratch=(), alias=None):
    used, skipped = len(args), len(args) + len(after)

    def run(*refs):
        kernel(*refs[:used], *refs[skipped:])

    return pl.pallas_call(
        run,
        in_specs=[*specs, *[pl.BlockSpec(memory_space=pl.ANY)] * len(after)],
        out_specs=[WHOLE] * len(outs),
        out_shape=outs,
        scratch_shapes=scratch,
        input_output_aliases=alias or {},
        cost_estimate=pl.CostEstimate(flops=0, bytes_accessed=0, transcendentals=0),
        compiler_params=pltpu.CompilerParams(vmem_limit_bytes=12 * MIB),
        name=name,
    )(*args, *after)


def array(rows, dtype):
    return jax.ShapeDtypeStruct((rows, 256), dtype)


def load(slot_values, after):
    return kernel_call(
        load_kernel,
        "load",
        [pl.BlockSpec(memory_space=pltpu.HBM)],
        (slot_values,),
        [
            jax.ShapeDtypeStruct(slot_values.shape, bf16),
            jax.ShapeDtypeStruct((16, 2048, 256), bf16),
        ],
        0,
        after,
        [pltpu.SemaphoreType.DMA],
    )


def densify(tiles, zeros, plan, live_count, after):
    (dense,) = kernel_call(
        densify_kernel,
        "densify",
        [SCALAR, SCALAR, WHOLE, WHOLE],
        (live_count.reshape(1), plan, tiles, zeros),
        [jax.ShapeDtypeStruct(zeros.shape, bf16)],
        0,
        after,
        [pltpu.VMEM((128, 128), f32)],
        {3: 0},
    )
    return dense


def column_sum(dense_ref, sources, rho):
    total = jnp.zeros((256, 256), f32)
    for half in range(2):
        total = total + lax.dot_general(
            dense_ref[rho, half * 1024 : half * 1024 + 1024, :],
            sources[half][:1024, :],
            (((0,), (0,)), ((), ())),
            preferred_element_type=f32,
        )
    return total


def row_sum(dense_ref, sources, q):
    total = jnp.zeros((512, 256), f32)
    for rho in range(16):
        ref, first = (sources[rho // 2], rho % 2 * 256) if rho < 8 else (sources[4], rho * 256 - 2048)
        total = total + jnp.dot(
            dense_ref[rho, q * 512 : (q + 1) * 512, :],
            ref[first : first + 256, :],
            preferred_element_type=f32,
        )
    return total


def out_far_kernel(dense_ref, *refs):
    for part in range(8):
        rows = slice(part * 256, part * 256 + 256)
        refs[2][rows, :] = column_sum(dense_ref, refs[:2], 8 + part).astype(bf16)


def out_near_kernel(dense_ref, *refs):
    for part in range(8):
        rows = slice(part % 2 * 256, part % 2 * 256 + 256)
        refs[2 + part // 2][rows, :] = column_sum(dense_ref, refs[:2], part)


def in_far_kernel(dense_ref, *refs):
    out_ref = refs[-1]
    for q in (0, 1):
        out_ref[q * 512 : q * 512 + 512, :] = row_sum(dense_ref, refs[:5], 2 + q).astype(bf16)
    if len(refs) == 7:
        out_ref[1024:, :] = refs[5][...]


def out_send_kernel(*refs):
    near, arrived, extra, own, outs = refs[:4], refs[4], refs[5:-4], refs[-4], refs[-3:]
    own[...] = near[0][...] + arrived[:512, :].astype(f32)
    for dy in (1, 2, 3):
        total = near[dy][...] + arrived[dy * 512 : dy * 512 + 512, :].astype(f32)
        outs[dy - 1][:512, :] = total.astype(bf16)
        for ref in extra:
            outs[dy - 1][512:, :] = ref[...]


def in_near_kernel(dense_ref, *refs):
    for q in (0, 1):
        refs[5][q * 512 : q * 512 + 512, :] = row_sum(dense_ref, refs[:5], q)


def join_kernel(*refs):
    for p in range(4):
        refs[4][p * 512 : p * 512 + 512, :] = refs[p][:512, :]


def pair_kernel(a_ref, b_ref, out_ref):
    out_ref[:256, :] = a_ref[:256, :]
    out_ref[256:512, :] = b_ref[:256, :]
    if a_ref.shape[0] > 256:
        total = a_ref[256:, :].astype(f32) + b_ref[256:, :].astype(f32)
        out_ref[512:, :] = total.astype(bf16)


def quad_kernel(a_ref, b_ref, c_ref, d_ref, out_ref):
    for k, ref in enumerate((a_ref, b_ref, c_ref, d_ref)):
        out_ref[k * 256 : k * 256 + 256, :] = ref[:256, :]
    if a_ref.shape[0] > 256:
        a, b, c, d = (ref[256:, :].astype(f32) for ref in (a_ref, b_ref, c_ref, d_ref))
        out_ref[1024:, :] = ((a + c) + (b + d)).astype(bf16)


def carry_kernel(kept_ref, core_ref, grad_in_ref, grad_out_ref, for_z, for_x):
    total = kept_ref[...] + core_ref[...].astype(f32)
    for_z[:256, :] = grad_out_ref[...]
    for_z[256:, :] = total[:128, :].astype(bf16)
    for_x[:256, :] = grad_in_ref[...]
    for_x[256:, :] = total[128:, :].astype(bf16)


def ring(value, move):
    return [value] + [move(value, -step) for step in (1, 2, 3)]


def propagate(dense, by_col, by_row, other, extra_y, extra_z):
    per_slice = 2 * 2048 * 256 * 256
    wide = [WHOLE] * 20
    sums = lambda kernel, name, args, outs, after=(): kernel_call(
        kernel, name, wide[: len(args)], args, outs, 8 * per_slice, after
    )
    (far,) = sums(out_far_kernel, "out_far", (dense, *by_col), [array(2048, bf16)], by_row[1:])
    arrived = row_move(far, 0, 0, 1)
    extra = lambda value: () if value is None else (value,)
    rows = lambda count, value: array(count if value is None else count + value.shape[0], bf16)
    (in_far,) = sums(
        in_far_kernel,
        "in_far",
        (dense, *by_row, other, *extra(extra_z)),
        [rows(1024, extra_z)],
        (far,),
    )
    in_other = col_move(in_far, 0, 1)
    near = sums(out_near_kernel, "out_near", (dense, *by_col), [array(512, f32)] * 4, (in_far,))
    out_own, *out_sent = sums(
        out_send_kernel,
        "out_send",
        (*near, arrived, *extra(extra_y)),
        [array(512, f32)] + [rows(512, extra_y)] * 3,
    )
    out_moved = [row_move(out_sent[dy - 1], 0, dy, 0) for dy in (1, 2, 3)]
    (in_near,) = sums(
        in_near_kernel, "in_near", (dense, *by_row, other), [array(1024, f32)], (out_own,)
    )
    in_own = in_near + in_other[:1024].astype(f32)
    out_total = out_own + sum_of([piece[:512] for piece in out_moved])
    return in_own, out_total, in_other[1024:], [piece[512:] for piece in out_moved]


def gather_x(in_own, extra):
    moved = [
        col_move(joined(in_own[dx * 256 : dx * 256 + 256].astype(bf16), extra), dx, 0) for dx in (1, 2, 3)
    ]
    return in_own[:256] + sum_of([piece[:256] for piece in moved]), [piece[256:] for piece in moved]


def joined(value, extra):
    return value if extra is None else jnp.concatenate([value, extra], axis=0)


def four(mine, others):
    one, two, three = (other.astype(f32) for other in others)
    return ((mine.astype(f32) + two) + (one + three)).astype(bf16)


def two(mine, other):
    return (mine.astype(f32) + other.astype(f32)).astype(bf16)


def sum_of(values):
    total = values[0].astype(f32)
    for value in values[1:]:
        total = total + value.astype(f32)
    return total


def middle_kernel(
    r_ref,
    in_total,
    out_own,
    out_last,
    weight_ref,
    cot_ref,
    hidden_ref,
    grad_in_ref,
    grad_out_ref,
    kept_ref,
    sent_ref,
    term,
):
    inbound = in_total[...].astype(bf16)
    outbound = (out_own[...] + out_last[...].astype(f32)).astype(bf16)
    width = inbound.shape[1]
    upper = weight_ref[:width, :]
    lower = weight_ref[width:, :]
    pre_act = jnp.dot(inbound, upper, preferred_element_type=f32)
    pre_act = pre_act + jnp.dot(outbound, lower, preferred_element_type=f32)
    sigma = jax.nn.sigmoid(pre_act)
    hidden_ref[...] = (pre_act * sigma).astype(bf16)
    slope = sigma * (1.0 + pre_act * (1.0 - sigma))
    grad_pre = (cot_ref[...].astype(f32) * slope).astype(bf16)
    across = (((1,), (1,)), ((), ()))
    grad_in_ref[...] = lax.dot_general(grad_pre, upper, across, preferred_element_type=f32).astype(bf16)
    grad_out = lax.dot_general(grad_pre, lower, across, preferred_element_type=f32)
    grad_out_ref[...] = grad_out.astype(bf16)
    down = (((0,), (0,)), ((), ()))
    term[:width, :] = lax.dot_general(inbound, grad_pre, down, preferred_element_type=f32)
    term[width:, :] = lax.dot_general(outbound, grad_pre, down, preferred_element_type=f32)
    core = r_ref[0] & 1
    kept_ref[...] = term[pl.ds(pl.multiple_of(core * 256, 256), 256), :]
    sent_ref[...] = term[pl.ds(pl.multiple_of((1 - core) * 256, 256), 256), :].astype(bf16)


def middle(r, terms, weight, cotangent):
    return kernel_call(
        middle_kernel,
        "middle",
        [SCALAR] + [WHOLE] * 5,
        (r, *terms, weight, cotangent),
        [array(256, bf16)] * 3 + [array(256, f32), array(256, bf16)],
        6 * 256 * 512 * 256,
        (),
        [pltpu.VMEM((512, 256), f32)],
    )


def place_kernel(r_ref, same_ref, other_ref, out_ref):
    core = r_ref[0] & 1
    out_ref[pl.ds(pl.multiple_of(core * 256, 256), 256), :] = same_ref[...].astype(f32)
    out_ref[pl.ds(pl.multiple_of((1 - core) * 256, 256), 256), :] = other_ref[...].astype(f32)


def body(features, tile_vals, tile_rows, tile_cols, tile_counts, combine_weight, cotangent):
    live_count = tile_counts[0, 0]
    r = lax.axis_index("row").astype(jnp.int32).reshape(1)
    plan = places(tile_rows[0, 0], tile_cols[0, 0], live_count)

    move_x = lambda value, step: col_move(value, step, 0)
    move_y = lambda value, step: row_move(value, 0, step, 0)
    plain = lambda kernel, name, args, outs, after=(): kernel_call(
        kernel, name, [WHOLE] * len(args), args, outs, 0, after
    )
    row_z = row_move(features, 1, 0, 0)
    (row_pair,) = plain(pair_kernel, "pair", (features, row_z), [array(512, bf16)])
    quads = ring(features, move_x)
    (quad,) = plain(quad_kernel, "quad", quads, [array(1024, bf16)], (row_z,))
    by_col = [quad, col_move(quad, 0, 1)]
    tiles, zeros = load(tile_vals[0, 0], (row_pair,))
    dense = densify(tiles, zeros, plan, live_count, (row_pair,))
    by_row = ring(row_pair, move_y)
    (joint,) = plain(join_kernel, "join", by_row, [array(2048, bf16)], (dense,))
    in_own, out_total, _, _ = propagate(dense, by_col, by_row, row_move(joint, 0, 0, 1), None, None)
    in_total, _ = gather_x(in_own, None)
    out_last = row_move(out_total[256:].astype(bf16), 1, 0, 0)
    terms = (in_total, out_total[:256], out_last)
    hidden, grad_in, grad_out, kept, sent = middle(r, terms, combine_weight, cotangent)

    for_z, for_x = plain(
        carry_kernel, "carry", (kept, row_move(sent, 0, 0, 1), grad_in, grad_out), [array(384, bf16)] * 2
    )
    row_z = row_move(for_z, 1, 0, 0)
    quads = ring(for_x, move_x)
    (quad,) = plain(quad_kernel, "quad_and", quads, [array(1152, bf16)], (row_z,))
    (row_pair,) = plain(pair_kernel, "pair_and", (for_z, row_z), [array(640, bf16)], (quad,))
    quad_z = col_move(quad, 0, 1)
    second = two(quad[1024:], quad_z[1024:])
    by_row = ring(row_pair, move_y)
    first = four(row_pair[512:], [piece[512:] for piece in by_row[1:]])
    joint = jnp.concatenate([piece[:512] for piece in by_row], axis=0)
    in_own, out_total, z_first, y_second = propagate(
        dense, [quad, quad_z], by_row, row_move(joint, 0, 0, 1), second, first
    )
    first = two(first, z_first)
    second = four(second, y_second)
    in_total, x_first = gather_x(in_own, first)
    first = four(first, x_first)
    out_last = row_move(jnp.concatenate([out_total[256:].astype(bf16), second], axis=0), 1, 0, 0)
    second = two(second, out_last[256:])
    same = jnp.concatenate([first, second], axis=0)
    (grad_weight,) = kernel_call(
        place_kernel,
        "place",
        [SCALAR, WHOLE, WHOLE],
        (r, same, row_move(same, 0, 0, 1)),
        [array(512, f32)],
        0,
    )
    grad_features = sum_of([in_total, out_total[:256], out_last[:256]]).astype(bf16)
    return hidden, grad_features, grad_weight


def solution(mesh):
    slabs = P(("row", "col"), None)
    return jax.shard_map(
        body,
        mesh=mesh,
        in_specs=(
            slabs,
            P("row", "col", None, None, None),
            P("row", "col", None),
            P("row", "col", None),
            P("row", "col"),
            P(),
            slabs,
        ),
        out_specs=(slabs, slabs, P()),
        check_vma=False,
    )
```

```python
import jax
import jax.numpy as jnp
from jax import lax
from jax.experimental import pallas as pl
from jax.experimental.pallas import tpu as pltpu
from jax.sharding import PartitionSpec as P

f32 = jnp.float32
bf16 = jnp.bfloat16
MIB = 1 << 20


def row_pairs(dz, dy, dc):
    return [
        (i, ((i >> 3) ^ dz) << 3 | (((i >> 1 & 3) + dy) % 4) << 1 | ((i & 1) ^ dc)) for i in range(16)
    ]


def col_pairs(dx, dz):
    return [(i, (((i >> 1) + dx) % 4) << 1 | ((i & 1) ^ dz)) for i in range(8)]


def row_move(value, dz, dy, dc):
    return lax.ppermute(value, "row", row_pairs(dz, dy, dc))


def col_move(value, dx, dz):
    return lax.ppermute(value, "col", col_pairs(dx, dz))


GROUP = 8


def places(tile_rows, tile_cols, live_count):
    r = lax.axis_index("row")
    c = lax.axis_index("col")
    slots = tile_rows.shape[0]
    slice_c = tile_rows >> 1
    slice_r = tile_cols >> 1
    kappa = ((slice_c ^ c) & 1) << 2 | (((slice_c >> 1) - (c >> 1)) & 3)
    rho = ((slice_r ^ r) & 1) << 3 | (((slice_r >> 1) - (r >> 1)) & 3) << 1 | (((slice_r ^ r) >> 3) & 1)
    key = rho << 5 | kappa << 2 | (tile_rows & 1) << 1 | (tile_cols & 1)
    index = jnp.arange(slots, dtype=jnp.int32)
    key = jnp.where(index < live_count, key, 512)
    unique = key * slots + index
    rank = jnp.sum((unique[None, :] < unique[:, None]).astype(jnp.int32), axis=1)
    hit = rank[:, None] == index[None, :]
    ordered = jnp.sum(jnp.where(hit, unique[:, None], 0), axis=0)
    order = ordered % slots
    place = ordered // slots
    again = jnp.concatenate([jnp.zeros((1,), jnp.int32), (place[1:] == place[:-1]).astype(jnp.int32)])
    return jnp.stack([order, place, again])


def load_kernel(vals_ref, tiles_ref, dense_ref, sem):
    copy = pltpu.make_async_copy(vals_ref, tiles_ref, sem)
    copy.start()

    @pl.loop(0, 16)
    def _(rho):
        dense_ref[rho] = jnp.zeros(dense_ref.shape[1:], bf16)

    copy.wait()


def densify_kernel(count_ref, plan_ref, tiles, zeros_ref, dense_ref, total, later):
    del zeros_ref
    count = count_ref[0]

    def put(k, value):
        place = plan_ref[1, k]
        at_row = pl.ds(pl.multiple_of(((place >> 1) & 15) * 128, 128), 128)
        at_col = pl.ds(pl.multiple_of((place & 1) * 128, 128), 128)
        dense_ref[place >> 5, at_row, at_col] = value

    def copy_group(group, found):
        for member in range(GROUP):
            k = jnp.minimum(group * GROUP + member, count - 1)
            put(k, tiles[plan_ref[0, k]])
            later[found] = k
            found = found + jnp.where(group * GROUP + member < count, plan_ref[2, k], 0)
        return found

    found = lax.fori_loop(0, (count + GROUP - 1) // GROUP, copy_group, 0)

    @pl.loop(0, found)
    def _(n):
        k = later[n]
        before = tiles[plan_ref[0, k - 1]].astype(f32)
        before = jnp.where(plan_ref[2, k - 1] == 1, total[...], before)
        now = before + tiles[plan_ref[0, k]].astype(f32)
        total[...] = now
        put(k, now.astype(bf16))


WHOLE = pl.BlockSpec(memory_space=pltpu.VMEM)
SCALAR = pl.BlockSpec(memory_space=pltpu.SMEM)


def kernel_call(kernel, name, specs, args, outs, flops, after=(), scratch=(), alias=None):
    used, skipped = len(args), len(args) + len(after)

    def run(*refs):
        kernel(*refs[:used], *refs[skipped:])

    return pl.pallas_call(
        run,
        in_specs=[*specs, *[pl.BlockSpec(memory_space=pl.ANY)] * len(after)],
        out_specs=[WHOLE] * len(outs),
        out_shape=outs,
        scratch_shapes=scratch,
        input_output_aliases=alias or {},
        cost_estimate=pl.CostEstimate(flops=0, bytes_accessed=0, transcendentals=0),
        compiler_params=pltpu.CompilerParams(vmem_limit_bytes=12 * MIB),
        name=name,
    )(*args, *after)


def array(rows, dtype):
    return jax.ShapeDtypeStruct((rows, 256), dtype)


def load(slot_values, after):
    return kernel_call(
        load_kernel,
        "load",
        [pl.BlockSpec(memory_space=pltpu.HBM)],
        (slot_values,),
        [
            jax.ShapeDtypeStruct(slot_values.shape, bf16),
            jax.ShapeDtypeStruct((16, 2048, 256), bf16),
        ],
        0,
        after,
        [pltpu.SemaphoreType.DMA],
    )


def densify(tiles, zeros, plan, live_count, after):
    (dense,) = kernel_call(
        densify_kernel,
        "densify",
        [SCALAR, SCALAR, WHOLE, WHOLE],
        (live_count.reshape(1), plan, tiles, zeros),
        [jax.ShapeDtypeStruct(zeros.shape, bf16)],
        0,
        after,
        [pltpu.VMEM((128, 128), f32), pltpu.SMEM((tiles.shape[0] + 8,), jnp.int32)],
        {3: 0},
    )
    return dense


def column_sum(dense_ref, sources, rho):
    total = jnp.zeros((256, 256), f32)
    for half in range(2):
        total = total + lax.dot_general(
            dense_ref[rho, half * 1024 : half * 1024 + 1024, :],
            sources[half][:1024, :],
            (((0,), (0,)), ((), ())),
            preferred_element_type=f32,
        )
    return total


def row_sum(dense_ref, sources, q):
    total = jnp.zeros((512, 256), f32)
    for rho in range(16):
        ref, first = (sources[(0, 2, 1, 3)[rho // 2]], rho % 2 * 256) if rho < 8 else (sources[4], rho * 256 - 2048)
        total = total + jnp.dot(
            dense_ref[rho, q * 512 : (q + 1) * 512, :],
            ref[first : first + 256, :],
            preferred_element_type=f32,
        )
    return total


def out_far_kernel(dense_ref, *refs):
    for part in range(8):
        rows = slice(part * 256, part * 256 + 256)
        refs[2][rows, :] = column_sum(dense_ref, refs[:2], 8 + part).astype(bf16)


def out_near_kernel(dense_ref, *refs):
    for part in range(8):
        rows = slice(part % 2 * 256, part % 2 * 256 + 256)
        refs[2 + part // 2][rows, :] = column_sum(dense_ref, refs[:2], part)


def in_far_kernel(dense_ref, *refs):
    for q in (0, 1):
        refs[5][q * 512 : q * 512 + 512, :] = row_sum(dense_ref, refs[:5], 2 + q).astype(bf16)


def out_send_kernel(*refs):
    near, arrived, own, outs = refs[:4], refs[4], refs[5], refs[6:]
    own[...] = near[0][...] + arrived[:512, :].astype(f32)
    for dy in (1, 2, 3):
        total = near[dy][...] + arrived[dy * 512 : dy * 512 + 512, :].astype(f32)
        outs[dy - 1][...] = total.astype(bf16)


def in_send_kernel(near_ref, arrived_ref, own_ref, *outs):
    for dx in range(4):
        rows = slice(dx * 256, dx * 256 + 256)
        total = near_ref[rows, :] + arrived_ref[rows, :].astype(f32)
        if dx == 0:
            own_ref[...] = total
        else:
            outs[dx - 1][...] = total.astype(bf16)


def in_near_kernel(dense_ref, *refs):
    for q in (0, 1):
        refs[5][q * 512 : q * 512 + 512, :] = row_sum(dense_ref, refs[:5], q)


def join_kernel(*refs):
    for p, ref in zip((0, 2, 1, 3), refs):
        refs[4][p * 512 : p * 512 + 512, :] = ref[:512, :]


def pair_kernel(a_ref, b_ref, out_ref):
    out_ref[:256, :] = a_ref[...]
    out_ref[256:, :] = b_ref[...]


def hold_kernel(value_ref, out_ref):
    out_ref[...] = value_ref[...]


def quad_kernel(a_ref, c_ref, b_ref, d_ref, out_ref):
    for k, ref in enumerate((a_ref, b_ref, c_ref, d_ref)):
        out_ref[k * 256 : k * 256 + 256, :] = ref[...]


def two_kernel(a_ref, b_ref, out_ref):
    out_ref[...] = (a_ref[...].astype(f32) + b_ref[...].astype(f32)).astype(bf16)


ORDER = (2, 1, 3)


def ring(value, move):
    moved = {step: move(value, -step) for step in ORDER}
    return [value, moved[1], moved[2], moved[3]]


def propagate(dense, by_col, by_row, other):
    per_slice = 2 * 2048 * 256 * 256
    by_row = [by_row[k] for k in (0, 2, 1, 3)]
    sums = lambda kernel, name, args, outs, after=(): kernel_call(
        kernel, name, [WHOLE] * len(args), args, outs, 8 * per_slice, after
    )
    (far,) = sums(out_far_kernel, "out_far", (dense, *by_col), [array(2048, bf16)], by_row[1:])
    arrived = row_move(far, 0, 0, 1)
    (in_far,) = sums(in_far_kernel, "in_far", (dense, *by_row, other), [array(1024, bf16)], (far,))
    in_other = col_move(in_far, 0, 1)
    near = sums(
        out_near_kernel, "out_near", (dense, *by_col), [array(512, f32)] * 4, (in_far,)
    )
    out_own, *out_sent = sums(
        out_send_kernel, "out_send", (*near, arrived), [array(512, f32)] + [array(512, bf16)] * 3
    )
    out_moved = [row_move(out_sent[dy - 1], 0, dy, 0) for dy in ORDER]
    (in_near,) = sums(
        in_near_kernel, "in_near", (dense, *by_row, other), [array(1024, f32)], (out_own,)
    )
    in_own, *in_sent = sums(
        in_send_kernel,
        "in_send",
        (in_near, in_other),
        [array(256, f32)] + [array(256, bf16)] * 3,
    )
    in_moved = [col_move(in_sent[dx - 1], dx, 0) for dx in ORDER]
    return in_own + sum_of(in_moved), out_own + sum_of(out_moved), (near[0], in_near, in_own)


def sum_of(values):
    total = values[0].astype(f32)
    for value in values[1:]:
        total = total + value.astype(f32)
    return total


def middle_kernel(
    r_ref,
    in_total,
    out_own,
    out_last,
    weight_ref,
    cot_ref,
    hidden_ref,
    grad_in_ref,
    grad_out_ref,
    kept_ref,
    sent_ref,
    term,
):
    inbound = in_total[...].astype(bf16)
    outbound = (out_own[...] + out_last[...].astype(f32)).astype(bf16)
    width = inbound.shape[1]
    upper = weight_ref[:width, :]
    lower = weight_ref[width:, :]
    pre_act = jnp.dot(inbound, upper, preferred_element_type=f32)
    pre_act = pre_act + jnp.dot(outbound, lower, preferred_element_type=f32)
    sigma = jax.nn.sigmoid(pre_act)
    hidden_ref[...] = (pre_act * sigma).astype(bf16)
    slope = sigma * (1.0 + pre_act * (1.0 - sigma))
    grad_pre = (cot_ref[...].astype(f32) * slope).astype(bf16)
    across = (((1,), (1,)), ((), ()))
    grad_in_ref[...] = lax.dot_general(grad_pre, upper, across, preferred_element_type=f32).astype(bf16)
    grad_out = lax.dot_general(grad_pre, lower, across, preferred_element_type=f32)
    grad_out_ref[...] = grad_out.astype(bf16)
    down = (((0,), (0,)), ((), ()))
    term[:width, :] = lax.dot_general(inbound, grad_pre, down, preferred_element_type=f32)
    term[width:, :] = lax.dot_general(outbound, grad_pre, down, preferred_element_type=f32)
    core = r_ref[0] & 1
    kept_ref[...] = term[pl.ds(pl.multiple_of(core * 256, 256), 256), :]
    sent_ref[...] = term[pl.ds(pl.multiple_of((1 - core) * 256, 256), 256), :].astype(bf16)


def middle(r, terms, weight, cotangent):
    return kernel_call(
        middle_kernel,
        "middle",
        [SCALAR] + [WHOLE] * 5,
        (r, *terms, weight, cotangent),
        [array(256, bf16)] * 3 + [array(256, f32), array(256, bf16)],
        6 * 256 * 512 * 256,
        (),
        [pltpu.VMEM((512, 256), f32)],
    )


def place_kernel(r_ref, same_ref, other_ref, out_ref):
    core = r_ref[0] & 1
    out_ref[pl.ds(pl.multiple_of(core * 256, 256), 256), :] = same_ref[...].astype(f32)
    out_ref[pl.ds(pl.multiple_of((1 - core) * 256, 256), 256), :] = other_ref[...].astype(f32)


def body(features, tile_vals, tile_rows, tile_cols, tile_counts, combine_weight, cotangent):
    live_count = tile_counts[0, 0]
    r = lax.axis_index("row").astype(jnp.int32).reshape(1)
    plan = places(tile_rows[0, 0], tile_cols[0, 0], live_count)

    move_x = lambda value, step: col_move(value, step, 0)
    move_y = lambda value, step: row_move(value, 0, step, 0)
    plain = lambda kernel, name, args, outs, after=(): kernel_call(
        kernel, name, [WHOLE] * len(args), args, outs, 0, after
    )
    row_z = row_move(features, 1, 0, 0)
    (held,) = plain(hold_kernel, "hold", (features,), [array(256, bf16)])
    (row_pair,) = plain(pair_kernel, "pair", (held, row_z), [array(512, bf16)])
    quads = ring(features, move_x)
    (quad,) = plain(quad_kernel, "quad", [held, quads[2], quads[1], quads[3]], [array(1024, bf16)], (row_z,))
    by_col = [quad, col_move(quad, 0, 1)]
    tiles, zeros = load(tile_vals[0, 0], (row_pair,))
    dense = densify(tiles, zeros, plan, live_count, (row_pair,))
    by_row = ring(row_pair, move_y)
    (joint,) = plain(join_kernel, "join", [by_row[k] for k in (0, 2, 1, 3)], [array(2048, bf16)], (dense,))
    in_total, out_total, _ = propagate(dense, by_col, by_row, row_move(joint, 0, 0, 1))
    out_last = row_move(out_total[256:].astype(bf16), 1, 0, 0)
    terms = (in_total, out_total[:256], out_last)
    hidden, grad_in, grad_out, kept, sent = middle(r, terms, combine_weight, cotangent)

    add = lambda a, b, name, *after: plain(two_kernel, name, (a, b), [array(256, bf16)], after)[0]
    swap_y = lambda value, bit: lax.ppermute(value, "row", [(i, i ^ bit << 1) for i in range(16)])
    swap_x = lambda value, bit: lax.ppermute(value, "col", [(i, i ^ bit << 1) for i in range(8)])
    part = add(kept, row_move(sent, 0, 0, 1), "sum_core")
    part_y = add(part, swap_y(part, 1), "sum_y1")
    part_z = add(part_y, row_move(part_y, 1, 0, 0), "sum_z2")
    part_x = add(part_z, swap_x(part_z, 1), "sum_x1")
    other_y = swap_y(part_x, 2)

    (held,) = plain(hold_kernel, "hold_and", (grad_out,), [array(256, bf16)], (part,))
    row_z = row_move(held, 1, 0, 0)
    quads = ring(grad_in, move_x)
    (quad,) = plain(
        quad_kernel, "quad_and", [quads[k] for k in (0, 2, 1, 3)], [array(1024, bf16)], (row_z,)
    )
    (row_pair,) = plain(pair_kernel, "pair_and", (held, row_z), [array(512, bf16)], (quad, part_y))
    by_row = ring(row_pair, move_y)
    (joint,) = plain(
        join_kernel, "join_and", [by_row[k] for k in (0, 2, 1, 3)], [array(2048, bf16)], (part_x,)
    )
    in_total, out_total, done = propagate(
        dense, [quad, col_move(quad, 0, 1)], by_row, row_move(joint, 0, 0, 1)
    )
    part_yy = add(part_x, other_y, "sum_y2", done[0])
    part_xx = add(part_yy, swap_x(part_yy, 2), "sum_x2", done[2])
    part_all = add(part_xx, col_move(part_xx, 0, 1), "sum_z1")
    out_last = row_move(out_total[256:].astype(bf16), 1, 0, 0)
    (grad_weight,) = kernel_call(
        place_kernel,
        "place",
        [SCALAR, WHOLE, WHOLE],
        (r, part_all, row_move(part_all, 0, 0, 1)),
        [array(512, f32)],
        0,
    )
    grad_features = sum_of([in_total, out_total[:256], out_last]).astype(bf16)
    return hidden, grad_features, grad_weight


def solution(mesh):
    slabs = P(("row", "col"), None)
    return jax.shard_map(
        body,
        mesh=mesh,
        in_specs=(
            slabs,
            P("row", "col", None, None, None),
            P("row", "col", None),
            P("row", "col", None),
            P("row", "col"),
            P(),
            slabs,
        ),
        out_specs=(slabs, slabs, P()),
        check_vma=False,
    )
```

```python
import jax
import jax.numpy as jnp
from jax import lax
from jax.experimental import pallas as pl
from jax.experimental.pallas import tpu as pltpu
from jax.sharding import PartitionSpec as P

f32 = jnp.float32
bf16 = jnp.bfloat16
MIB = 1 << 20


def row_pairs(dz, dy, dc):
    return [
        (i, ((i >> 3) ^ dz) << 3 | ((i >> 1 & 3) ^ dy) << 1 | ((i & 1) ^ dc)) for i in range(16)
    ]


def col_pairs(dx, dz):
    return [(i, ((i >> 1) ^ dx) << 1 | ((i & 1) ^ dz)) for i in range(8)]


def row_move(value, dz, dy, dc):
    return lax.ppermute(value, "row", row_pairs(dz, dy, dc))


def col_move(value, dx, dz):
    return lax.ppermute(value, "col", col_pairs(dx, dz))


GROUP = 8


def places(tile_rows, tile_cols, live_count):
    r = lax.axis_index("row")
    c = lax.axis_index("col")
    slots = tile_rows.shape[0]
    slice_c = tile_rows >> 1
    slice_r = tile_cols >> 1
    kappa = ((slice_c ^ c) & 1) << 2 | (((slice_c >> 1) ^ (c >> 1)) & 3)
    rho = ((slice_r ^ r) & 1) << 3 | (((slice_r >> 1) ^ (r >> 1)) & 3) << 1 | (((slice_r ^ r) >> 3) & 1)
    key = rho << 5 | kappa << 2 | (tile_rows & 1) << 1 | (tile_cols & 1)
    index = jnp.arange(slots, dtype=jnp.int32)
    key = jnp.where(index < live_count, key, 512)
    unique = key * slots + index
    rank = jnp.sum((unique[None, :] < unique[:, None]).astype(jnp.int32), axis=1)
    hit = rank[:, None] == index[None, :]
    ordered = jnp.sum(jnp.where(hit, unique[:, None], 0), axis=0)
    order = ordered % slots
    place = ordered // slots
    again = jnp.concatenate([jnp.zeros((1,), jnp.int32), (place[1:] == place[:-1]).astype(jnp.int32)])
    return jnp.stack([order, place, again])


def load_kernel(vals_ref, tiles_ref, dense_ref, sem):
    copy = pltpu.make_async_copy(vals_ref, tiles_ref, sem)
    copy.start()

    @pl.loop(0, 16)
    def _(rho):
        dense_ref[rho] = jnp.zeros(dense_ref.shape[1:], bf16)

    copy.wait()


def densify_kernel(count_ref, plan_ref, tiles, zeros_ref, dense_ref, total, later):
    del zeros_ref
    count = count_ref[0]

    def put(k, value):
        place = plan_ref[1, k]
        at_row = pl.ds(pl.multiple_of(((place >> 1) & 15) * 128, 128), 128)
        at_col = pl.ds(pl.multiple_of((place & 1) * 128, 128), 128)
        dense_ref[place >> 5, at_row, at_col] = value

    def copy_group(group, found):
        for member in range(GROUP):
            k = jnp.minimum(group * GROUP + member, count - 1)
            put(k, tiles[plan_ref[0, k]])
            later[found] = k
            found = found + jnp.where(group * GROUP + member < count, plan_ref[2, k], 0)
        return found

    found = lax.fori_loop(0, (count + GROUP - 1) // GROUP, copy_group, 0)

    @pl.loop(0, found)
    def _(n):
        k = later[n]
        before = tiles[plan_ref[0, k - 1]].astype(f32)
        before = jnp.where(plan_ref[2, k - 1] == 1, total[...], before)
        now = before + tiles[plan_ref[0, k]].astype(f32)
        total[...] = now
        put(k, now.astype(bf16))


WHOLE = pl.BlockSpec(memory_space=pltpu.VMEM)
SCALAR = pl.BlockSpec(memory_space=pltpu.SMEM)


def kernel_call(kernel, name, specs, args, outs, flops, after=(), scratch=(), alias=None):
    used, skipped = len(args), len(args) + len(after)

    def run(*refs):
        kernel(*refs[:used], *refs[skipped:])

    return pl.pallas_call(
        run,
        in_specs=[*specs, *[pl.BlockSpec(memory_space=pl.ANY)] * len(after)],
        out_specs=[WHOLE] * len(outs),
        out_shape=outs,
        scratch_shapes=scratch,
        input_output_aliases=alias or {},
        cost_estimate=pl.CostEstimate(flops=0, bytes_accessed=0, transcendentals=0),
        compiler_params=pltpu.CompilerParams(vmem_limit_bytes=12 * MIB),
        name=name,
    )(*args, *after)


def array(rows, dtype):
    return jax.ShapeDtypeStruct((rows, 256), dtype)


def load(slot_values, after):
    return kernel_call(
        load_kernel,
        "load",
        [pl.BlockSpec(memory_space=pltpu.HBM)],
        (slot_values,),
        [
            jax.ShapeDtypeStruct(slot_values.shape, bf16),
            jax.ShapeDtypeStruct((16, 2048, 256), bf16),
        ],
        0,
        after,
        [pltpu.SemaphoreType.DMA],
    )


def densify(tiles, zeros, plan, live_count, after):
    (dense,) = kernel_call(
        densify_kernel,
        "densify",
        [SCALAR, SCALAR, WHOLE, WHOLE],
        (live_count.reshape(1), plan, tiles, zeros),
        [jax.ShapeDtypeStruct(zeros.shape, bf16)],
        0,
        after,
        [pltpu.VMEM((128, 128), f32), pltpu.SMEM((tiles.shape[0] + 8,), jnp.int32)],
        {3: 0},
    )
    return dense


def column_sum(dense_ref, sources, rho):
    total = jnp.zeros((256, 256), f32)
    for half in range(2):
        total = total + lax.dot_general(
            dense_ref[rho, half * 1024 : half * 1024 + 1024, :],
            sources[half][:1024, :],
            (((0,), (0,)), ((), ())),
            preferred_element_type=f32,
        )
    return total


def row_sum(dense_ref, sources, q):
    total = jnp.zeros((512, 256), f32)
    for rho in range(16):
        ref, first = (sources[(0, 1, 3, 2)[rho // 2]], rho % 2 * 256) if rho < 8 else (sources[4], rho * 256 - 2048)
        total = total + jnp.dot(
            dense_ref[rho, q * 512 : (q + 1) * 512, :],
            ref[first : first + 256, :],
            preferred_element_type=f32,
        )
    return total


def out_far_kernel(dense_ref, *refs):
    for part in range(8):
        rows = slice(part * 256, part * 256 + 256)
        refs[2][rows, :] = column_sum(dense_ref, refs[:2], 8 + part).astype(bf16)


def out_near_kernel(dense_ref, *refs):
    for part in range(2, 8):
        rows = slice(part % 2 * 256, part % 2 * 256 + 256)
        refs[1 + part // 2][rows, :] = column_sum(dense_ref, refs[:2], part)


def in_far_kernel(dense_ref, *refs):
    for q in (0, 1):
        refs[5][q * 512 : q * 512 + 512, :] = row_sum(dense_ref, refs[:5], 2 + q).astype(bf16)


def out_send_kernel(*refs):
    near, arrived, outs = refs[:3], refs[3], refs[4:]
    for dy in (1, 2, 3):
        total = near[dy - 1][...] + arrived[dy * 512 : dy * 512 + 512, :].astype(f32)
        outs[dy - 1][...] = total.astype(bf16)


def in_send_kernel(near_ref, arrived_ref, own_ref, *outs):
    for dx in range(4):
        rows = slice(dx * 256, dx * 256 + 256)
        total = near_ref[rows, :] + arrived_ref[rows, :].astype(f32)
        if dx == 0:
            own_ref[...] = total
        else:
            outs[dx - 1][...] = total.astype(bf16)


def own_kernel(dense_ref, *refs):
    by_col, by_row, arrived, in_near, out_own = refs[:2], refs[2:7], refs[7], refs[8], refs[9]
    for q in (0, 1):
        in_near[q * 512 : q * 512 + 512, :] = row_sum(dense_ref, by_row, q)
    for part in (0, 1):
        rows = slice(part * 256, part * 256 + 256)
        out_own[rows, :] = column_sum(dense_ref, by_col, part) + arrived[rows, :].astype(f32)


def join_kernel(*refs):
    for p, ref in zip((0, 1, 3, 2), refs):
        refs[4][p * 512 : p * 512 + 512, :] = ref[:512, :]


def pair_kernel(a_ref, b_ref, out_ref):
    out_ref[:256, :] = a_ref[...]
    out_ref[256:, :] = b_ref[...]


def hold_kernel(value_ref, out_ref):
    out_ref[...] = value_ref[...]


def quad_kernel(a_ref, b_ref, d_ref, c_ref, out_ref):
    for k, ref in enumerate((a_ref, b_ref, c_ref, d_ref)):
        out_ref[k * 256 : k * 256 + 256, :] = ref[...]


def two_kernel(a_ref, b_ref, out_ref):
    out_ref[...] = (a_ref[...].astype(f32) + b_ref[...].astype(f32)).astype(bf16)


ORDER = (2, 1, 3)


def ring(value, move):
    moved = {step: move(value, step) for step in ORDER}
    return [value, moved[1], moved[2], moved[3]]


def propagate(dense, by_col, by_row, other):
    per_slice = 2 * 2048 * 256 * 256
    by_row = [by_row[k] for k in (0, 1, 3, 2)]
    sums = lambda kernel, name, args, outs, after=(): kernel_call(
        kernel, name, [WHOLE] * len(args), args, outs, 8 * per_slice, after
    )
    (far,) = sums(out_far_kernel, "out_far", (dense, *by_col), [array(2048, bf16)], by_row[1:])
    arrived = row_move(far, 0, 0, 1)
    (in_far,) = sums(in_far_kernel, "in_far", (dense, *by_row, other), [array(1024, bf16)], (far,))
    in_other = col_move(in_far, 0, 1)
    near = sums(
        out_near_kernel, "out_near", (dense, *by_col), [array(512, f32)] * 3, (in_far,)
    )
    out_sent = sums(out_send_kernel, "out_send", (*near, arrived), [array(512, bf16)] * 3)
    out_moved = [row_move(out_sent[dy - 1], 0, dy, 0) for dy in ORDER]
    in_near, out_own = sums(
        own_kernel,
        "own",
        (dense, *by_col, *by_row, other, arrived),
        [array(1024, f32), array(512, f32)],
        out_sent[:1],
    )
    in_own, *in_sent = sums(
        in_send_kernel,
        "in_send",
        (in_near, in_other),
        [array(256, f32)] + [array(256, bf16)] * 3,
    )
    in_moved = [col_move(in_sent[dx - 1], dx, 0) for dx in ORDER]
    return in_own + sum_of(in_moved), out_own + sum_of(out_moved), (near[0], in_near, in_own)


def sum_of(values):
    total = values[0].astype(f32)
    for value in values[1:]:
        total = total + value.astype(f32)
    return total


def middle_kernel(
    r_ref,
    in_total,
    out_own,
    out_last,
    weight_ref,
    cot_ref,
    hidden_ref,
    grad_in_ref,
    grad_out_ref,
    kept_ref,
    sent_ref,
    term,
):
    inbound = in_total[...].astype(bf16)
    outbound = (out_own[...] + out_last[...].astype(f32)).astype(bf16)
    width = inbound.shape[1]
    upper = weight_ref[:width, :]
    lower = weight_ref[width:, :]
    pre_act = jnp.dot(inbound, upper, preferred_element_type=f32)
    pre_act = pre_act + jnp.dot(outbound, lower, preferred_element_type=f32)
    sigma = jax.nn.sigmoid(pre_act)
    hidden_ref[...] = (pre_act * sigma).astype(bf16)
    slope = sigma * (1.0 + pre_act * (1.0 - sigma))
    grad_pre = (cot_ref[...].astype(f32) * slope).astype(bf16)
    across = (((1,), (1,)), ((), ()))
    grad_in_ref[...] = lax.dot_general(grad_pre, upper, across, preferred_element_type=f32).astype(bf16)
    grad_out = lax.dot_general(grad_pre, lower, across, preferred_element_type=f32)
    grad_out_ref[...] = grad_out.astype(bf16)
    down = (((0,), (0,)), ((), ()))
    term[:width, :] = lax.dot_general(inbound, grad_pre, down, preferred_element_type=f32)
    term[width:, :] = lax.dot_general(outbound, grad_pre, down, preferred_element_type=f32)
    core = r_ref[0] & 1
    kept_ref[...] = term[pl.ds(pl.multiple_of(core * 256, 256), 256), :]
    sent_ref[...] = term[pl.ds(pl.multiple_of((1 - core) * 256, 256), 256), :].astype(bf16)


def middle(r, terms, weight, cotangent):
    return kernel_call(
        middle_kernel,
        "middle",
        [SCALAR] + [WHOLE] * 5,
        (r, *terms, weight, cotangent),
        [array(256, bf16)] * 3 + [array(256, f32), array(256, bf16)],
        6 * 256 * 512 * 256,
        (),
        [pltpu.VMEM((512, 256), f32)],
    )


def place_kernel(r_ref, same_ref, other_ref, out_ref):
    core = r_ref[0] & 1
    out_ref[pl.ds(pl.multiple_of(core * 256, 256), 256), :] = same_ref[...].astype(f32)
    out_ref[pl.ds(pl.multiple_of((1 - core) * 256, 256), 256), :] = other_ref[...].astype(f32)


def body(features, tile_vals, tile_rows, tile_cols, tile_counts, combine_weight, cotangent):
    live_count = tile_counts[0, 0]
    r = lax.axis_index("row").astype(jnp.int32).reshape(1)
    plan = places(tile_rows[0, 0], tile_cols[0, 0], live_count)

    move_x = lambda value, step: col_move(value, step, 0)
    move_y = lambda value, step: row_move(value, 0, step, 0)
    plain = lambda kernel, name, args, outs, after=(): kernel_call(
        kernel, name, [WHOLE] * len(args), args, outs, 0, after
    )
    row_z = row_move(features, 1, 0, 0)
    (held,) = plain(hold_kernel, "hold", (features,), [array(256, bf16)])
    (row_pair,) = plain(pair_kernel, "pair", (held, row_z), [array(512, bf16)])
    quads = ring(features, move_x)
    (quad,) = plain(quad_kernel, "quad", [held, quads[1], quads[3], quads[2]], [array(1024, bf16)], (row_z,))
    by_col = [quad, col_move(quad, 0, 1)]
    tiles, zeros = load(tile_vals[0, 0], (row_pair,))
    dense = densify(tiles, zeros, plan, live_count, (row_pair,))
    by_row = ring(row_pair, move_y)
    (joint,) = plain(join_kernel, "join", [by_row[k] for k in (0, 1, 3, 2)], [array(2048, bf16)], (dense,))
    in_total, out_total, _ = propagate(dense, by_col, by_row, row_move(joint, 0, 0, 1))
    out_last = row_move(out_total[256:].astype(bf16), 1, 0, 0)
    terms = (in_total, out_total[:256], out_last)
    hidden, grad_in, grad_out, kept, sent = middle(r, terms, combine_weight, cotangent)

    add = lambda a, b, name, *after: plain(two_kernel, name, (a, b), [array(256, bf16)], after)[0]
    swap_y = lambda value, bit: lax.ppermute(value, "row", [(i, i ^ bit << 1) for i in range(16)])
    swap_x = lambda value, bit: lax.ppermute(value, "col", [(i, i ^ bit << 1) for i in range(8)])
    part = add(kept, row_move(sent, 0, 0, 1), "sum_core")
    part_y = add(part, swap_y(part, 2), "sum_y")
    part_z = add(part_y, row_move(part_y, 1, 0, 0), "sum_z2")
    part_x = add(part_z, swap_x(part_z, 2), "sum_x")
    other_y = swap_y(part_x, 1)

    (held,) = plain(hold_kernel, "hold_and", (grad_out,), [array(256, bf16)], (part,))
    row_z = row_move(held, 1, 0, 0)
    quads = ring(grad_in, move_x)
    (quad,) = plain(
        quad_kernel, "quad_and", [quads[k] for k in (0, 1, 3, 2)], [array(1024, bf16)], (row_z,)
    )
    (row_pair,) = plain(pair_kernel, "pair_and", (held, row_z), [array(512, bf16)], (quad, part_y))
    by_row = ring(row_pair, move_y)
    (joint,) = plain(
        join_kernel, "join_and", [by_row[k] for k in (0, 1, 3, 2)], [array(2048, bf16)], (part_x,)
    )
    in_total, out_total, done = propagate(
        dense, [quad, col_move(quad, 0, 1)], by_row, row_move(joint, 0, 0, 1)
    )
    part_yy = add(part_x, other_y, "sum_yy", done[0])
    part_xx = add(part_yy, swap_x(part_yy, 1), "sum_xx", done[2])
    part_all = add(part_xx, col_move(part_xx, 0, 1), "sum_z1")
    out_last = row_move(out_total[256:].astype(bf16), 1, 0, 0)
    (grad_weight,) = kernel_call(
        place_kernel,
        "place",
        [SCALAR, WHOLE, WHOLE],
        (r, part_all, row_move(part_all, 0, 0, 1)),
        [array(512, f32)],
        0,
    )
    grad_features = sum_of([in_total, out_total[:256], out_last]).astype(bf16)
    return hidden, grad_features, grad_weight


def solution(mesh):
    slabs = P(("row", "col"), None)
    return jax.shard_map(
        body,
        mesh=mesh,
        in_specs=(
            slabs,
            P("row", "col", None, None, None),
            P("row", "col", None),
            P("row", "col", None),
            P("row", "col"),
            P(),
            slabs,
        ),
        out_specs=(slabs, slabs, P()),
        check_vma=False,
    )
```

```python
import jax
import jax.numpy as jnp
from jax import lax
from jax.experimental import pallas as pl
from jax.experimental.pallas import tpu as pltpu
from jax.sharding import PartitionSpec as P

f32 = jnp.float32
bf16 = jnp.bfloat16
MIB = 1 << 20


def row_pairs(dz, dy, dc):
    return [
        (i, ((i >> 3) ^ dz) << 3 | ((i >> 1 & 3) ^ dy) << 1 | ((i & 1) ^ dc)) for i in range(16)
    ]


def col_pairs(dx, dz):
    return [(i, ((i >> 1) ^ dx) << 1 | ((i & 1) ^ dz)) for i in range(8)]


def row_move(value, dz, dy, dc):
    return lax.ppermute(value, "row", row_pairs(dz, dy, dc))


def col_move(value, dx, dz):
    return lax.ppermute(value, "col", col_pairs(dx, dz))


GROUP = 8


def places(tile_rows, tile_cols, live_count):
    r = lax.axis_index("row")
    c = lax.axis_index("col")
    slots = tile_rows.shape[0]
    slice_c = tile_rows >> 1
    slice_r = tile_cols >> 1
    kappa = ((slice_c ^ c) & 1) << 2 | (((slice_c >> 1) ^ (c >> 1)) & 3)
    rho = ((slice_r ^ r) & 1) << 3 | (((slice_r >> 1) ^ (r >> 1)) & 3) << 1 | (((slice_r ^ r) >> 3) & 1)
    key = rho << 5 | kappa << 2 | (tile_rows & 1) << 1 | (tile_cols & 1)
    index = jnp.arange(slots, dtype=jnp.int32)
    key = jnp.where(index < live_count, key, 512)
    unique = key * slots + index
    rank = jnp.sum((unique[None, :] < unique[:, None]).astype(jnp.int32), axis=1)
    hit = rank[:, None] == index[None, :]
    ordered = jnp.sum(jnp.where(hit, unique[:, None], 0), axis=0)
    order = ordered % slots
    place = ordered // slots
    again = jnp.concatenate([jnp.zeros((1,), jnp.int32), (place[1:] == place[:-1]).astype(jnp.int32)])
    return jnp.stack([order, place, again])


def load_kernel(vals_ref, tiles_ref, dense_ref, sem):
    copy = pltpu.make_async_copy(vals_ref, tiles_ref, sem)
    copy.start()

    @pl.loop(0, 16)
    def _(rho):
        dense_ref[rho] = jnp.zeros(dense_ref.shape[1:], bf16)

    copy.wait()


def densify_kernel(count_ref, plan_ref, tiles, zeros_ref, dense_ref, total, later):
    del zeros_ref
    count = count_ref[0]

    def put(k, value):
        place = plan_ref[1, k]
        at_row = pl.ds(pl.multiple_of(((place >> 1) & 15) * 128, 128), 128)
        at_col = pl.ds(pl.multiple_of((place & 1) * 128, 128), 128)
        dense_ref[place >> 5, at_row, at_col] = value

    def copy_group(group, found):
        for member in range(GROUP):
            k = jnp.minimum(group * GROUP + member, count - 1)
            put(k, tiles[plan_ref[0, k]])
            later[found] = k
            found = found + jnp.where(group * GROUP + member < count, plan_ref[2, k], 0)
        return found

    found = lax.fori_loop(0, (count + GROUP - 1) // GROUP, copy_group, 0)

    @pl.loop(0, found)
    def _(n):
        k = later[n]
        before = tiles[plan_ref[0, k - 1]].astype(f32)
        before = jnp.where(plan_ref[2, k - 1] == 1, total[...], before)
        now = before + tiles[plan_ref[0, k]].astype(f32)
        total[...] = now
        put(k, now.astype(bf16))


WHOLE = pl.BlockSpec(memory_space=pltpu.VMEM)
SCALAR = pl.BlockSpec(memory_space=pltpu.SMEM)


def kernel_call(kernel, name, specs, args, outs, flops, after=(), scratch=(), alias=None):
    used, skipped = len(args), len(args) + len(after)

    def run(*refs):
        kernel(*refs[:used], *refs[skipped:])

    return pl.pallas_call(
        run,
        in_specs=[*specs, *[pl.BlockSpec(memory_space=pl.ANY)] * len(after)],
        out_specs=[WHOLE] * len(outs),
        out_shape=outs,
        scratch_shapes=scratch,
        input_output_aliases=alias or {},
        cost_estimate=pl.CostEstimate(flops=0, bytes_accessed=0, transcendentals=0),
        compiler_params=pltpu.CompilerParams(vmem_limit_bytes=12 * MIB),
        name=name,
    )(*args, *after)


def array(rows, dtype):
    return jax.ShapeDtypeStruct((rows, 256), dtype)


def load(slot_values, after):
    return kernel_call(
        load_kernel,
        "load",
        [pl.BlockSpec(memory_space=pltpu.HBM)],
        (slot_values,),
        [
            jax.ShapeDtypeStruct(slot_values.shape, bf16),
            jax.ShapeDtypeStruct((16, 2048, 256), bf16),
        ],
        0,
        after,
        [pltpu.SemaphoreType.DMA],
    )


def densify(tiles, zeros, plan, live_count, after):
    (dense,) = kernel_call(
        densify_kernel,
        "densify",
        [SCALAR, SCALAR, WHOLE, WHOLE],
        (live_count.reshape(1), plan, tiles, zeros),
        [jax.ShapeDtypeStruct(zeros.shape, bf16)],
        0,
        after,
        [pltpu.VMEM((128, 128), f32), pltpu.SMEM((tiles.shape[0] + 8,), jnp.int32)],
        {3: 0},
    )
    return dense


def column_sum(dense_ref, sources, rho):
    total = jnp.zeros((256, 256), f32)
    for half in range(2):
        total = total + lax.dot_general(
            dense_ref[rho, half * 1024 : half * 1024 + 1024, :],
            sources[half][:1024, :],
            (((0,), (0,)), ((), ())),
            preferred_element_type=f32,
        )
    return total


def row_sum(dense_ref, sources, q):
    total = jnp.zeros((512, 256), f32)
    for rho in range(16):
        ref, first = (sources[(0, 1, 3, 2)[rho // 2]], rho % 2 * 256) if rho < 8 else (sources[4], rho * 256 - 2048)
        total = total + jnp.dot(
            dense_ref[rho, q * 512 : (q + 1) * 512, :],
            ref[first : first + 256, :],
            preferred_element_type=f32,
        )
    return total


def out_far_kernel(dense_ref, *refs):
    for part in range(8):
        rows = slice(part * 256, part * 256 + 256)
        refs[2][rows, :] = column_sum(dense_ref, refs[:2], 8 + part).astype(bf16)


def out_near_kernel(dense_ref, *refs):
    for part in range(2, 8):
        rows = slice(part % 2 * 256, part % 2 * 256 + 256)
        refs[1 + part // 2][rows, :] = column_sum(dense_ref, refs[:2], part)


def in_far_kernel(dense_ref, *refs):
    for q in (0, 1):
        refs[5][q * 512 : q * 512 + 512, :] = row_sum(dense_ref, refs[:5], 2 + q).astype(bf16)


def out_send_kernel(*refs):
    near, arrived, outs = refs[:3], refs[3], refs[4:]
    for dy in (1, 2, 3):
        total = near[dy - 1][...] + arrived[dy * 512 : dy * 512 + 512, :].astype(f32)
        outs[dy - 1][...] = total.astype(bf16)


def in_send_kernel(near_ref, arrived_ref, own_ref, *outs):
    for dx in range(4):
        rows = slice(dx * 256, dx * 256 + 256)
        total = near_ref[rows, :] + arrived_ref[rows, :].astype(f32)
        if dx == 0:
            own_ref[...] = total
        else:
            outs[dx - 1][...] = total.astype(bf16)


def own_kernel(dense_ref, *refs):
    by_col, by_row, arrived, in_near, out_own = refs[:2], refs[2:7], refs[7], refs[8], refs[9]
    for q in (0, 1):
        in_near[q * 512 : q * 512 + 512, :] = row_sum(dense_ref, by_row, q)
    for part in (0, 1):
        rows = slice(part * 256, part * 256 + 256)
        out_own[rows, :] = column_sum(dense_ref, by_col, part) + arrived[rows, :].astype(f32)


def join_kernel(*refs):
    for p, ref in zip((0, 1, 3, 2), refs):
        refs[4][p * 512 : p * 512 + 512, :] = ref[:512, :]


def pair_kernel(a_ref, b_ref, out_ref):
    out_ref[:256, :] = a_ref[...]
    out_ref[256:, :] = b_ref[...]


def hold_kernel(value_ref, out_ref):
    out_ref[...] = value_ref[...]


def quad_kernel(a_ref, b_ref, d_ref, c_ref, out_ref):
    for k, ref in enumerate((a_ref, b_ref, c_ref, d_ref)):
        out_ref[k * 256 : k * 256 + 256, :] = ref[...]


def two_kernel(a_ref, b_ref, out_ref):
    out_ref[...] = (a_ref[...].astype(f32) + b_ref[...].astype(f32)).astype(bf16)


ORDER = (2, 1, 3)


def ring(value, move):
    moved = {step: move(value, step) for step in ORDER}
    return [value, moved[1], moved[2], moved[3]]


def propagate(dense, by_col, by_row, other):
    per_slice = 2 * 2048 * 256 * 256
    by_row = [by_row[k] for k in (0, 1, 3, 2)]
    sums = lambda kernel, name, args, outs, after=(): kernel_call(
        kernel, name, [WHOLE] * len(args), args, outs, 8 * per_slice, after
    )
    (far,) = sums(out_far_kernel, "out_far", (dense, *by_col), [array(2048, bf16)], by_row[1:])
    arrived = row_move(far, 0, 0, 1)
    (in_far,) = sums(in_far_kernel, "in_far", (dense, *by_row, other), [array(1024, bf16)], (far,))
    in_other = col_move(in_far, 0, 1)
    near = sums(
        out_near_kernel, "out_near", (dense, *by_col), [array(512, f32)] * 3, (in_far,)
    )
    out_sent = sums(out_send_kernel, "out_send", (*near, arrived), [array(512, bf16)] * 3)
    out_moved = [row_move(out_sent[dy - 1], 0, dy, 0) for dy in ORDER]
    in_near, out_own = sums(
        own_kernel,
        "own",
        (dense, *by_col, *by_row, other, arrived),
        [array(1024, f32), array(512, f32)],
        out_sent[:1],
    )
    in_own, *in_sent = sums(
        in_send_kernel,
        "in_send",
        (in_near, in_other),
        [array(256, f32)] + [array(256, bf16)] * 3,
    )
    in_moved = [col_move(in_sent[dx - 1], dx, 0) for dx in ORDER]
    return in_own + sum_of(in_moved), out_own + sum_of(out_moved), (near[0], in_near, in_own)


def sum_of(values):
    total = values[0].astype(f32)
    for value in values[1:]:
        total = total + value.astype(f32)
    return total


def middle_kernel(
    r_ref,
    in_total,
    out_own,
    out_last,
    weight_ref,
    cot_ref,
    hidden_ref,
    grad_in_ref,
    grad_out_ref,
    kept_ref,
    sent_ref,
    term,
):
    inbound = in_total[...].astype(bf16)
    outbound = (out_own[...] + out_last[...].astype(f32)).astype(bf16)
    width = inbound.shape[1]
    upper = weight_ref[:width, :]
    lower = weight_ref[width:, :]
    pre_act = jnp.dot(inbound, upper, preferred_element_type=f32)
    pre_act = pre_act + jnp.dot(outbound, lower, preferred_element_type=f32)
    sigma = jax.nn.sigmoid(pre_act)
    hidden_ref[...] = (pre_act * sigma).astype(bf16)
    slope = sigma * (1.0 + pre_act * (1.0 - sigma))
    grad_pre = (cot_ref[...].astype(f32) * slope).astype(bf16)
    across = (((1,), (1,)), ((), ()))
    grad_in_ref[...] = lax.dot_general(grad_pre, upper, across, preferred_element_type=f32).astype(bf16)
    grad_out = lax.dot_general(grad_pre, lower, across, preferred_element_type=f32)
    grad_out_ref[...] = grad_out.astype(bf16)
    down = (((0,), (0,)), ((), ()))
    term[:width, :] = lax.dot_general(inbound, grad_pre, down, preferred_element_type=f32)
    term[width:, :] = lax.dot_general(outbound, grad_pre, down, preferred_element_type=f32)
    core = r_ref[0] & 1
    kept_ref[...] = term[pl.ds(pl.multiple_of(core * 256, 256), 256), :]
    sent_ref[...] = term[pl.ds(pl.multiple_of((1 - core) * 256, 256), 256), :].astype(bf16)


def middle(r, terms, weight, cotangent):
    return kernel_call(
        middle_kernel,
        "middle",
        [SCALAR] + [WHOLE] * 5,
        (r, *terms, weight, cotangent),
        [array(256, bf16)] * 3 + [array(256, f32), array(256, bf16)],
        6 * 256 * 512 * 256,
        (),
        [pltpu.VMEM((512, 256), f32)],
    )


def place_kernel(r_ref, same_ref, other_ref, out_ref):
    core = r_ref[0] & 1
    out_ref[pl.ds(pl.multiple_of(core * 256, 256), 256), :] = same_ref[...].astype(f32)
    out_ref[pl.ds(pl.multiple_of((1 - core) * 256, 256), 256), :] = other_ref[...].astype(f32)


def body(features, tile_vals, tile_rows, tile_cols, tile_counts, combine_weight, cotangent):
    live_count = tile_counts[0, 0]
    r = lax.axis_index("row").astype(jnp.int32).reshape(1)
    plan = places(tile_rows[0, 0], tile_cols[0, 0], live_count)

    move_x = lambda value, step: col_move(value, step, 0)
    move_y = lambda value, step: row_move(value, 0, step, 0)
    plain = lambda kernel, name, args, outs, after=(): kernel_call(
        kernel, name, [WHOLE] * len(args), args, outs, 0, after
    )
    row_z = row_move(features, 1, 0, 0)
    (held,) = plain(hold_kernel, "hold", (features,), [array(256, bf16)])
    (row_pair,) = plain(pair_kernel, "pair", (held, row_z), [array(512, bf16)])
    quads = ring(features, move_x)
    (quad,) = plain(quad_kernel, "quad", [held, quads[1], quads[3], quads[2]], [array(1024, bf16)], (row_z,))
    by_col = [quad, col_move(quad, 0, 1)]
    tiles, zeros = load(tile_vals[0, 0], (row_pair,))
    dense = densify(tiles, zeros, plan, live_count, (row_pair,))
    by_row = ring(row_pair, move_y)
    (joint,) = plain(join_kernel, "join", [by_row[k] for k in (0, 1, 3, 2)], [array(2048, bf16)], (dense,))
    in_total, out_total, _ = propagate(dense, by_col, by_row, row_move(joint, 0, 0, 1))
    out_last = row_move(out_total[256:].astype(bf16), 1, 0, 0)
    terms = (in_total, out_total[:256], out_last)
    hidden, grad_in, grad_out, kept, sent = middle(r, terms, combine_weight, cotangent)

    add = lambda a, b, name, *after: plain(two_kernel, name, (a, b), [array(256, bf16)], after)[0]
    swap_y = lambda value, bit: lax.ppermute(value, "row", [(i, i ^ bit << 1) for i in range(16)])
    swap_x = lambda value, bit: lax.ppermute(value, "col", [(i, i ^ bit << 1) for i in range(8)])
    part = add(kept, row_move(sent, 0, 0, 1), "sum_core")
    part_y = add(part, swap_y(part, 2), "sum_y")
    part_z = add(part_y, row_move(part_y, 1, 0, 0), "sum_z2")
    part_x = add(part_z, swap_x(part_z, 2), "sum_x")
    other_x = swap_x(part_x, 1)

    (held,) = plain(hold_kernel, "hold_and", (grad_out,), [array(256, bf16)], (part,))
    row_z = row_move(held, 1, 0, 0)
    quads = ring(grad_in, move_x)
    (quad,) = plain(
        quad_kernel, "quad_and", [quads[k] for k in (0, 1, 3, 2)], [array(1024, bf16)], (row_z,)
    )
    (row_pair,) = plain(pair_kernel, "pair_and", (held, row_z), [array(512, bf16)], (quad, part_y))
    by_row = ring(row_pair, move_y)
    (joint,) = plain(
        join_kernel, "join_and", [by_row[k] for k in (0, 1, 3, 2)], [array(2048, bf16)], (part_x,)
    )
    in_total, out_total, done = propagate(
        dense, [quad, col_move(quad, 0, 1)], by_row, row_move(joint, 0, 0, 1)
    )
    part_xx = add(part_x, other_x, "sum_xx", done[0])
    part_zz = add(part_xx, col_move(part_xx, 0, 1), "sum_z1", done[2])
    part_all = add(part_zz, swap_y(part_zz, 1), "sum_yy")
    out_last = row_move(out_total[256:].astype(bf16), 1, 0, 0)
    (grad_weight,) = kernel_call(
        place_kernel,
        "place",
        [SCALAR, WHOLE, WHOLE],
        (r, part_all, row_move(part_all, 0, 0, 1)),
        [array(512, f32)],
        0,
    )
    grad_features = sum_of([in_total, out_total[:256], out_last]).astype(bf16)
    return hidden, grad_features, grad_weight


def solution(mesh):
    slabs = P(("row", "col"), None)
    return jax.shard_map(
        body,
        mesh=mesh,
        in_specs=(
            slabs,
            P("row", "col", None, None, None),
            P("row", "col", None),
            P("row", "col", None),
            P("row", "col"),
            P(),
            slabs,
        ),
        out_specs=(slabs, slabs, P()),
        check_vma=False,
    )
```
